512 devices in a mesh: section: 8 (over y), fsdp: 8 (over z), dp: 8 (over x, core).
Axes of the slice: x: 4, y: 8, z: 8, core: 2. Of those that a mesh axis runs over, the one named last changes fastest.
Arguments:
- tokens_in: bfloat16 [4, 64, 128, 1664], P(None, ('fsdp', 'dp')), may hold values from -6 to 6
- keep_one: int32 [4, 64, 96], P(None, ('fsdp', 'dp')), may hold values from 0 to 127, as said below
- keep_two: int32 [4, 64, 64], P(None, ('fsdp', 'dp')), may hold values from 0 to 95, as said below
- keep_three: int32 [4, 64, 48], P(None, ('fsdp', 'dp')), may hold values from 0 to 63, as said below
- norm_gain: float32 [8, 1664], P('section'), may hold values from 0.5 to 1.5
- layer_scale: float32 [8, 1664], P('section'), may hold values from 0.3 to 1
- w_qkv: bfloat16 [8, 2496, 1664], P('section', ('fsdp', 'dp')), may hold values from -1 to 1
- w_out: bfloat16 [8, 832, 1664], P('section', ('fsdp', 'dp')), may hold values from -0.21875 to 0.21875
Outputs:
- stash: bfloat16 [8, 4, 64, 128, 1664], P('section', None, ('fsdp', 'dp'))
The draws below stay inside these ranges and needn't reach their ends.
Inputs may be any that keep to these rules, and one draw needn't show every extreme that they name: `keep_one`: each list is strictly increasing. `keep_two`: each list is strictly increasing. `keep_three`: each list is strictly increasing.
All inputs are finite; a program needn't handle non-finite values.
Results may differ from the reference program's by a relative error of at most 0.015.
Values may be sent and summed in bfloat16 or wider, within the bound.
A program may use at most 128 MiB of HBM per device.

```python
import jax
import jax.numpy as jnp
from jax import lax

F = 1664
HEADS = 13
HDIM = 64
HW = 832
TOK0 = 128
K1 = 96
K2 = 64
K3 = 48
MICRO = 4
SECTIONS = 8
IMAGES = 64
N_SECTION = 8


def pick_sorted(key, total, count):
    keys = jax.random.split(key, MICRO * IMAGES)
    orders = jax.vmap(lambda single: jax.random.permutation(single, total))(keys)
    chosen = jnp.sort(orders[:, :count], axis=-1)
    return chosen.reshape(MICRO, IMAGES, count).astype(jnp.int32)


def draw_keep_one(key, part):
    key = jax.random.fold_in(key, 1)
    return pick_sorted(key, TOK0, K1)


def draw_keep_two(key, part):
    key = jax.random.fold_in(key, 2)
    return pick_sorted(key, K1, K2)


def draw_keep_three(key, part):
    key = jax.random.fold_in(key, 3)
    return pick_sorted(key, K2, K3)


def draw_w_qkv(key, part):
    key = jax.random.fold_in(key, 11)
    width = HEADS * HDIM
    full = jnp.clip(jax.random.normal(key, (SECTIONS, 3 * width, F), jnp.float32), -4.0, 4.0) * F ** (-0.5)
    return full.astype(jnp.bfloat16)


def levels(stream_key, extent, shards, least, top_value):
    loudness = 1.0
    for position, blocks in shards:
        draws = jax.random.uniform(jax.random.fold_in(jax.random.fold_in(stream_key, 6), position), (blocks,), jnp.float32, least / len(shards), top_value / len(shards))
        loudness = loudness * jnp.repeat(jnp.exp(draws), extent[position] // blocks).reshape((-1,) + (1,) * (len(extent) - 1 - position))
    return loudness


def noise(key, shape, scale, limit, cuts=(), dtype=jnp.bfloat16):
    level = levels(key, shape, cuts, -0.22, 0.18) if cuts else 1.0
    entries = jax.random.normal(key, shape, jnp.float32) * scale * level
    return jnp.minimum(jnp.maximum(entries, -limit), limit).astype(dtype)


def setup_inputs(seed: int = 0) -> dict:
    arg_keys = jax.random.split(jax.random.key(seed), 9)
    return {
        "tokens_in": noise(arg_keys[0], (MICRO, IMAGES, TOK0, F), 1.0, 6.0, ((1, 64),)),
        "keep_one": draw_keep_one(jax.random.fold_in(arg_keys[8], 71), 0),
        "keep_two": draw_keep_two(jax.random.fold_in(arg_keys[8], 71), 0),
        "keep_three": draw_keep_three(jax.random.fold_in(arg_keys[8], 71), 0),
        "norm_gain": jnp.clip(1.0 + 0.1 * jax.random.normal(arg_keys[4], (SECTIONS, F), jnp.float32), 0.5, 1.5),
        "layer_scale": jnp.clip(0.3 + 0.7 * jax.random.uniform(arg_keys[5], (SECTIONS, F), jnp.float32) ** levels(arg_keys[5], (SECTIONS, F), ((0, 8),), -0.2, 0.2), 0.3, 1.0),
        "w_qkv": draw_w_qkv(jax.random.fold_in(arg_keys[8], 71), 0),
        "w_out": noise(arg_keys[7], (SECTIONS, HW, F), HW ** -0.5, 0.21875, ((0, 8), (1, 64))),
    }


EPS = 1e-06

def norm_rows(tokens, gain):
    values = tokens.astype(jnp.float32)
    center = values - lax.optimization_barrier(jnp.mean(values, axis=-1, keepdims=True))
    spread = lax.optimization_barrier(jnp.mean(center * center, axis=-1, keepdims=True))
    return (center * lax.rsqrt(spread + EPS) * gain).astype(jnp.bfloat16)

def attend(tokens, gain, scale, proj_in, proj_out):
    count = tokens.shape[0]
    rows = tokens.shape[1]
    width = proj_out.shape[0]
    heads = width // HDIM
    normed = norm_rows(tokens, gain)
    qkv = jnp.einsum('nkf,cf->nkc', normed.astype(jnp.float32), proj_in.astype(jnp.float32)).astype(jnp.bfloat16)
    query = qkv[:, :, :width].reshape(count, rows, heads, HDIM).astype(jnp.float32)
    keys = qkv[:, :, width:2 * width].reshape(count, rows, heads, HDIM).astype(jnp.float32)
    values = qkv[:, :, 2 * width:].reshape(count, rows, heads, HDIM).astype(jnp.float32)
    scores = jnp.einsum('nqhd,nkhd->nhqk', query, keys) * HDIM ** (-0.5)
    top = lax.optimization_barrier(jnp.max(scores, axis=-1, keepdims=True))
    expo = jnp.exp(scores - top)
    weights = (expo / lax.optimization_barrier(jnp.sum(expo, axis=-1, keepdims=True))).astype(jnp.bfloat16)
    mixed = jnp.einsum('nhqk,nkhd->nqhd', weights.astype(jnp.float32), values).astype(jnp.bfloat16)
    mixed = mixed.reshape(count, rows, width)
    branch = jnp.einsum('nkc,cf->nkf', mixed.astype(jnp.float32), proj_out.astype(jnp.float32))
    return (tokens.astype(jnp.float32) + scale * branch).astype(jnp.bfloat16)

def reference(tokens_in, keep_one, keep_two, keep_three, norm_gain, layer_scale, w_qkv, w_out):
    micro = tokens_in.shape[0]
    images = tokens_in.shape[1]
    total = tokens_in.shape[2]
    tokens = tokens_in.reshape(micro * images, total, tokens_in.shape[3])
    picks = [keep_one, keep_two, keep_three]
    layers = []
    for level in range(N_SECTION):
        for depth in range(3):
            if (depth + 1) * N_SECTION // 4 == level:
                chosen = picks[depth].reshape(micro * images, -1).astype(jnp.int32)
                tokens = jnp.take_along_axis(tokens, chosen[:, :, None], axis=1)
        tokens = attend(tokens, norm_gain[level], layer_scale[level], w_qkv[level], w_out[level])
        padded = jnp.pad(tokens, ((0, 0), (0, total - tokens.shape[1]), (0, 0)))
        layers.append(padded.reshape(micro, images, total, -1))
    return jnp.stack(layers, axis=0)
```

```python
import functools

import jax
import jax.numpy as jnp
import numpy as np
from jax import lax
from jax.experimental import pallas as pl
from jax.experimental.pallas import tpu as pltpu
from jax.sharding import PartitionSpec as P

MESH = pl.DeviceIdType.MESH
HDIM = 64
EPS = 1e-06
LANE = 128
MAIN = 48
REST = 64
A_ROWS = 272
A_HALF = 144
B_HALF = 208


def compaction(rows_in, rows_out, tiles):
    pad_in = -(-8 * rows_in // 16) * 16
    pad_out = -(-8 * rows_out // 16) * 16
    first = MAIN - rows_in
    left = rows_out - first
    every = np.zeros((pad_in + pad_out, 8 * MAIN + 8 * left), np.float32)
    rest = np.zeros((tiles * 8 * left, 8 * REST), np.float32)
    for core in range(2):
        for x in range(4):
            place, rank = core * 4 + x, x * 2 + core
            for i in range(rows_in):
                every[rank * rows_in + i, place * MAIN + i] = 1
            for i in range(first):
                every[pad_in + rank * rows_out + i, place * MAIN + rows_in + i] = 1
            for i in range(left):
                every[pad_in + rank * rows_out + first + i, 8 * MAIN + place * left + i] = 1
                for tile in range(tiles):
                    rest[tile * 8 * left + place * left + i, place * REST + tile * left + i] = 1
    return every, rest


def kernel(
    tok_ref,
    one_ref,
    two_ref,
    three_ref,
    gain_ref,
    scale_ref,
    wq_ref,
    wo_ref,
    every_ref,
    rest_ref,
    out_ref,
    gbuf,
    wd,
    wod,
    recv,
    res,
    pruned,
    picks,
    stage,
    small,
    normed,
    qkv,
    mixed,
    tok_sem,
    out_sem,
    z_send,
    z_recv,
    xa_send,
    xa_recv,
    xb_send,
    xb_recv,
    sib_send,
    sib_recv,
    t_send,
    t_recv,
):
    micro, rows, feats = tok_ref.shape
    tiles = feats // LANE
    rows_in, rows_out = wq_ref.shape[0], wo_ref.shape[0]
    group_in, group_out = 8 * rows_in, 8 * rows_out
    width = 64 * rows_out
    heads = width // HDIM
    left = rows_in + rows_out - MAIN
    level = lax.axis_index("section")
    z = lax.axis_index("fsdp")
    dp = lax.axis_index("dp")
    x = dp // 2
    core = dp - 2 * x

    def zat(step):
        return lax.rem(z + step + 8, 8)

    def xat(step):
        return lax.rem(x + step + 4, 4)

    x_plus, x_minus = (level, z, xat(1) * 2 + core), (level, z, xat(-1) * 2 + core)
    z_plus, z_minus = (level, zat(1), dp), (level, zat(-1), dp)
    sibling = (level, z, x * 2 + 1 - core)
    y_plus, y_minus = (lax.rem(level + 1, 8), z, dp), (lax.rem(level + 7, 8), z, dp)

    recv[...] = jnp.zeros_like(recv)
    barrier = pltpu.get_barrier_semaphore()
    partners = (x_plus, x_minus, z_plus, z_minus, sibling, y_plus, y_minus)
    for partner in partners:
        pl.semaphore_signal(barrier, inc=1, device_id=partner, device_id_type=MESH)

    stage[pl.ds(0, rows_in), :] = wq_ref[...].astype(jnp.float32)
    stage[pl.ds(rows_in, rows_out), :] = wo_ref[...].astype(jnp.float32)
    small[...] = jnp.zeros_like(small)
    for tile in range(tiles):
        lanes = slice(tile * LANE, (tile + 1) * LANE)
        gbuf[core, z, x, tile * MAIN : (tile + 1) * MAIN, :] = stage[0:MAIN, lanes].astype(jnp.bfloat16)
        small[tile * left : (tile + 1) * left, :] = stage[MAIN : MAIN + left, lanes]
    gbuf[core, z, x, tiles * MAIN : tiles * MAIN + REST, :] = small[...].astype(jnp.bfloat16)

    pl.semaphore_wait(barrier, len(partners))

    total = tiles * MAIN + REST
    A, A1, A2 = pl.ds(0, A_ROWS), pl.ds(0, A_HALF), pl.ds(A_HALF, A_ROWS - A_HALF)
    B, B1, B2 = (
        pl.ds(A_ROWS, total - A_ROWS),
        pl.ds(A_ROWS, B_HALF),
        pl.ds(A_ROWS + B_HALF, total - A_ROWS - B_HALF),
    )

    started = []

    def send(part, ss, rs, to):
        copy = pltpu.make_async_remote_copy(
            src_ref=part, dst_ref=part, send_sem=ss, recv_sem=rs, device_id=to, device_id_type=MESH
        )
        copy.start()
        started.append(copy)

    def arrive(part, ss, rs):
        pltpu.make_async_remote_copy(
            src_ref=part, dst_ref=part, send_sem=ss, recv_sem=rs, device_id=z_plus, device_id_type=MESH
        ).wait_recv()

    zdir = (z_plus, z_minus)
    xdir = (x_plus, x_minus)
    sign = (-1, 1)

    def at(dz, dx, part):
        return gbuf.at[core, zat(dz), xat(dx), part]

    def row(dz, part):
        return gbuf.at[core, zat(dz), :, part]

    def z_go(kind, d, k, part):
        send(part, z_send.at[kind, d, k - 1], z_recv.at[kind, d, k - 1], zdir[d])

    def z_come(kind, d, k, part):
        arrive(part, z_send.at[kind, d, k - 1], z_recv.at[kind, d, k - 1])

    def xa_go(d, k, part):
        send(part, xa_send.at[d, k - 1], xa_recv.at[d, k - 1], xdir[d])

    def xa_come(d, k, part):
        arrive(part, xa_send.at[d, k - 1], xa_recv.at[d, k - 1])

    def xb_go(dz, d, k, part):
        i = dz % 8
        send(part, xb_send.at[i, d, k - 1], xb_recv.at[i, d, k - 1], xdir[d])

    def xb_come(dz, d, k, part):
        i = dz % 8
        arrive(part, xb_send.at[i, d, k - 1], xb_recv.at[i, d, k - 1])

    def x_spread(dz):
        for d in range(2):
            xb_go(dz, d, 1, at(dz, 0, B))

    def x_relay(dz):
        for d in range(2):
            xb_come(dz, d, 1, at(dz, sign[d], B))
            xb_go(dz, d, 2, at(dz, sign[d], (B1, B2)[d]))

    def x_end(dz):
        for d in range(2):
            xb_come(dz, d, 2, at(dz, 2 * sign[d], (B1, B2)[d]))

    def to_sibling(dz):
        i = dz % 8
        send(gbuf.at[core, zat(dz)], sib_send.at[i], sib_recv.at[i], sibling)

    def pack(dz):
        i = dz % 8
        g = zat(dz)
        arrive(gbuf.at[1 - core, g], sib_send.at[i], sib_recv.at[i])
        tail = gbuf[:, g, :, tiles * MAIN : tiles * MAIN + REST, :].reshape(8 * REST, LANE)
        tail = jnp.dot(rest_ref[...], tail, preferred_element_type=jnp.float32).astype(jnp.bfloat16)
        for tile in range(0, tiles, 2):
            count = min(2, tiles - tile)
            columns = [
                jnp.concatenate(
                    [
                        gbuf[:, g, :, t * MAIN : (t + 1) * MAIN, :].reshape(8 * MAIN, LANE),
                        tail[t * 8 * left : (t + 1) * 8 * left, :],
                    ],
                    axis=0,
                )
                for t in range(tile, tile + count)
            ]
            block = columns[0] if count == 1 else jnp.concatenate(columns, axis=1)
            dense = jnp.dot(every_ref[...], block, preferred_element_type=jnp.float32).astype(jnp.bfloat16)
            lanes = slice(tile * LANE, (tile + count) * LANE)
            pad_in = wd.shape[1]
            wd[g, :, lanes] = dense[:pad_in]
            wod[g, :, lanes] = dense[pad_in:]

    for d in range(2):
        z_go(1, d, 1, at(0, 0, B))
    for d in range(2):
        xa_go(d, 1, at(0, 0, A))
    x_spread(0)

    @pl.when(level == 0)
    def _():
        pltpu.make_async_copy(tok_ref, recv, tok_sem).start()

    picks[...] = jnp.zeros_like(picks)
    for here, chosen in ((1, one_ref), (3, two_ref), (5, three_ref)):

        @pl.when(level == here)
        def _():
            count = chosen.shape[1]
            place = lax.broadcasted_iota(jnp.int32, (rows, count), 0)
            for m in range(micro):
                hit = place == chosen[m : m + 1, :]
                picks[m, :, 0:count] = jnp.where(hit, 1.0, 0.0).astype(jnp.bfloat16)

    for d in range(2):
        xa_come(d, 1, at(0, sign[d], A))
        xa_go(d, 2, at(0, sign[d], (A1, A2)[d]))

    def z_relay(k):
        for d in range(2):
            if k < 4:
                z_come(1, d, k, at(sign[d] * k, 0, B))
                z_go(1, d, k + 1, at(sign[d] * k, 0, B if k < 3 else (B1, B2)[d]))
                x_spread(sign[d] * k)
            else:
                z_come(1, d, k, at(4, 0, (B1, B2)[d]))
        if k == 4:
            x_spread(4)

    def za_relay(k):
        for d in range(2):
            if k < 4:
                z_come(0, d, k, row(sign[d] * k, A))
                z_go(0, d, k + 1, row(sign[d] * k, A if k < 3 else (A1, A2)[d]))
            else:
                z_come(0, d, k, row(4, (A1, A2)[d]))

    z_relay(1)
    x_relay(0)
    for d in range(2):
        xa_come(d, 2, at(0, 2, (A1, A2)[d]))
    for d in range(2):
        z_go(0, d, 1, row(0, A))
    z_relay(2)
    x_relay(-1)
    x_relay(1)
    z_relay(3)
    za_relay(1)
    x_relay(-2)
    x_relay(2)
    z_relay(4)
    x_end(0)
    to_sibling(0)
    za_relay(2)
    x_relay(-3)
    x_relay(3)
    x_end(-1)
    x_end(1)
    to_sibling(-1)
    to_sibling(1)
    pack(0)
    za_relay(3)
    x_relay(4)
    x_end(-2)
    x_end(2)
    to_sibling(-2)
    to_sibling(2)
    pack(-1)
    pack(1)
    x_end(-3)
    x_end(3)
    to_sibling(-3)
    to_sibling(3)
    pack(-2)
    pack(2)
    za_relay(4)
    x_end(4)
    to_sibling(4)
    pack(-3)
    pack(3)
    pack(4)

    live = rows - 32 * (level >= 2).astype(jnp.int32)
    live = live - 32 * (level >= 4).astype(jnp.int32) - 16 * (level >= 6).astype(jnp.int32)

    def token_copy(m, source, count):
        return pltpu.make_async_remote_copy(
            src_ref=source.at[m, pl.ds(0, count)],
            dst_ref=recv.at[m, pl.ds(0, count)],
            send_sem=t_send.at[m],
            recv_sem=t_recv.at[m],
            device_id=y_plus,
            device_id_type=MESH,
        )

    @pl.when(level == 0)
    def _():
        pltpu.make_async_copy(tok_ref, recv, tok_sem).wait()

    counts = (one_ref.shape[1], two_ref.shape[1], three_ref.shape[1])
    incoming = ((1, 1, rows), (2, 3, counts[0]), (4, 5, counts[1]), (6, 7, counts[2]))

    def body(m, carry):
        for low, high, count in incoming:

            @pl.when(jnp.logical_and(level >= low, level <= high))
            def _():
                token_copy(m, recv, count).wait_recv()

        values = recv[m].astype(jnp.float32)
        center = values - jnp.mean(values, axis=-1, keepdims=True)
        spread = jnp.mean(center * center, axis=-1, keepdims=True)
        normed[...] = (center * lax.rsqrt(spread + EPS) * gain_ref[...]).astype(jnp.bfloat16)

        def project(g, carry):
            part = lax.dot_general(
                wd[g], normed[...], (((1,), (1,)), ((), ())), preferred_element_type=jnp.float32
            )
            start = pl.multiple_of(g * group_in, 8)
            qkv[pl.ds(start, group_in), :] = part[:group_in]
            return carry

        lax.fori_loop(0, 8, project, 0)

        inside = lax.broadcasted_iota(jnp.int32, (rows, rows), 0) < live
        for h in range(heads):
            low = h * HDIM
            query = (qkv[low : low + HDIM, :].astype(jnp.bfloat16) * jnp.bfloat16(HDIM**-0.5))
            keys = qkv[width + low : width + low + HDIM, :].astype(jnp.bfloat16)
            vals = qkv[2 * width + low : 2 * width + low + HDIM, :].astype(jnp.bfloat16)
            scores = lax.dot_general(
                keys, query, (((0,), (0,)), ((), ())), preferred_element_type=jnp.float32
            )
            scores = jnp.where(inside, scores, -1e30)
            top = jnp.max(scores, axis=0, keepdims=True)
            expo = jnp.exp(scores - top)
            weights = (expo / jnp.sum(expo, axis=0, keepdims=True)).astype(jnp.bfloat16)
            mixed[low : low + HDIM, :] = jnp.dot(vals, weights, preferred_element_type=jnp.float32)

        parts = []
        gap = jnp.zeros((wod.shape[1] - group_out, rows), jnp.float32)
        for g in range(8):
            parts.append(mixed[g * group_out : (g + 1) * group_out, :])
            if gap.shape[0]:
                parts.append(gap)
        across = jnp.transpose(jnp.concatenate(parts, axis=0)).astype(jnp.bfloat16)
        alive = lax.broadcasted_iota(jnp.int32, (rows, LANE), 0) < live
        for low in range(0, feats, 4 * LANE):
            size = min(4 * LANE, feats - low)
            lanes = slice(low, low + size)
            block = wod[:, :, lanes].reshape(8 * wod.shape[1], size)
            branch = jnp.dot(across, block, preferred_element_type=jnp.float32)
            sums = recv[m, :, lanes].astype(jnp.float32) + scale_ref[:, lanes] * branch
            sums = jnp.where(alive[:, :1], sums, 0.0)
            res[m, :, lanes] = sums.astype(jnp.bfloat16)

        pltpu.make_async_copy(res.at[m], out_ref.at[m], out_sem.at[m]).start()

        for here, count in ((0, rows), (2, counts[0]), (4, counts[1]), (6, counts[2])):

            @pl.when(level == here)
            def _():
                token_copy(m, res, count).start()

        for here, count in ((1, counts[0]), (3, counts[1]), (5, counts[2])):

            @pl.when(level == here)
            def _():
                for low in range(0, feats, 4 * LANE):
                    size = min(4 * LANE, feats - low)
                    lanes = slice(low, low + size)
                    taken = lax.dot_general(
                        picks[m],
                        res[m, :, lanes],
                        (((0,), (0,)), ((), ())),
                        preferred_element_type=jnp.float32,
                    )
                    pruned[m, :, lanes] = taken.astype(jnp.bfloat16)
                token_copy(m, pruned, count).start()

        return carry

    lax.fori_loop(0, micro, body, 0)

    for copy in started:
        copy.wait_send()

    def finish(m, carry):
        pltpu.make_async_copy(res.at[m], out_ref.at[m], out_sem.at[m]).wait()
        for here, count in ((0, rows), (2, counts[0]), (4, counts[1]), (6, counts[2])):

            @pl.when(level == here)
            def _():
                token_copy(m, res, count).wait_send()

        for here, count in ((1, counts[0]), (3, counts[1]), (5, counts[2])):

            @pl.when(level == here)
            def _():
                token_copy(m, pruned, count).wait_send()

        return carry

    lax.fori_loop(0, micro, finish, 0)


def shards(tokens_in, keep_one, keep_two, keep_three, norm_gain, layer_scale, w_qkv, w_out):
    micro, _, rows, feats = tokens_in.shape
    rows_in, rows_out = w_qkv.shape[1], w_out.shape[1]
    tiles = feats // LANE
    every, rest = compaction(rows_in, rows_out, tiles)
    pad_in = -(-8 * rows_in // 16) * 16
    pad_out = -(-8 * rows_out // 16) * 16
    vmem = pl.BlockSpec(memory_space=pltpu.VMEM)
    dma = pltpu.SemaphoreType.DMA
    stash = pl.pallas_call(
        kernel,
        out_shape=jax.ShapeDtypeStruct((micro, rows, feats), jnp.bfloat16),
        in_specs=[pl.BlockSpec(memory_space=pl.ANY)] + [vmem] * 9,
        out_specs=pl.BlockSpec(memory_space=pl.ANY),
        scratch_shapes=[
            pltpu.VMEM((2, 8, 4, tiles * MAIN + REST, LANE), jnp.bfloat16),
            pltpu.VMEM((8, pad_in, feats), jnp.bfloat16),
            pltpu.VMEM((8, pad_out, feats), jnp.bfloat16),
            pltpu.VMEM((micro, rows, feats), jnp.bfloat16),
            pltpu.VMEM((micro, rows, feats), jnp.bfloat16),
            pltpu.VMEM((micro, rows, feats), jnp.bfloat16),
            pltpu.VMEM((micro, rows, rows), jnp.bfloat16),
            pltpu.VMEM((64, feats), jnp.float32),
            pltpu.VMEM((REST, LANE), jnp.float32),
            pltpu.VMEM((rows, feats), jnp.bfloat16),
            pltpu.VMEM((64 * rows_in, rows), jnp.float32),
            pltpu.VMEM((64 * rows_out, rows), jnp.float32),
            dma,
            dma((micro,)),
            dma((2, 2, 4)),
            dma((2, 2, 4)),
            dma((2, 2)),
            dma((2, 2)),
            dma((8, 2, 2)),
            dma((8, 2, 2)),
            dma((8,)),
            dma((8,)),
            dma((micro,)),
            dma((micro,)),
        ],
        compiler_params=pltpu.CompilerParams(
            collective_id=0, has_side_effects=True, vmem_limit_bytes=60 * 1024 * 1024
        ),
    )(
        tokens_in[:, 0],
        keep_one[:, 0],
        keep_two[:, 0],
        keep_three[:, 0],
        norm_gain,
        layer_scale,
        w_qkv[0],
        w_out[0],
        jnp.asarray(every, jnp.bfloat16),
        jnp.asarray(rest, jnp.bfloat16),
    )
    return stash[None, :, None]


def solution(mesh):
    return jax.shard_map(
        shards,
        mesh=mesh,
        in_specs=(
            P(None, ("fsdp", "dp"), None, None),
            P(None, ("fsdp", "dp"), None),
            P(None, ("fsdp", "dp"), None),
            P(None, ("fsdp", "dp"), None),
            P("section", None),
            P("section", None),
            P("section", ("fsdp", "dp"), None),
            P("section", ("fsdp", "dp"), None),
        ),
        out_specs=P("section", None, ("fsdp", "dp"), None, None),
        check_vma=False,
    )
```

```python
import heapq

import jax
import jax.numpy as jnp
import numpy as np
from jax import lax
from jax.experimental import pallas as pl
from jax.experimental.pallas import tpu as pltpu
from jax.sharding import PartitionSpec as P

MESH = pl.DeviceIdType.MESH
HDIM = 64
EPS = 1e-06
LANE = 128
MAIN = 48
REST = 64
A_ROWS = 272
A_HALF = 144
B_HALF = 208
TOTAL = 13 * MAIN + REST
LAST = {"x": 2, "z": 4}
SIGN = (-1, 1)
FIRST = (("B", "z"), ("A", "x"), ("A", "z"), ("B", "x"))


def compaction(rows_in, rows_out, tiles):
    pad_in = -(-8 * rows_in // 16) * 16
    pad_out = -(-8 * rows_out // 16) * 16
    first = MAIN - rows_in
    left = rows_out - first
    every = np.zeros((pad_in + pad_out, 8 * MAIN + 8 * left), np.float32)
    rest = np.zeros((tiles * 8 * left, 8 * REST), np.float32)
    for core in range(2):
        for x in range(4):
            place, rank = core * 4 + x, x * 2 + core
            for i in range(rows_in):
                every[rank * rows_in + i, place * MAIN + i] = 1
            for i in range(first):
                every[pad_in + rank * rows_out + i, place * MAIN + rows_in + i] = 1
            for i in range(left):
                every[pad_in + rank * rows_out + first + i, 8 * MAIN + place * left + i] = 1
                for tile in range(tiles):
                    rest[tile * 8 * left + place * left + i, place * REST + tile * left + i] = 1
    return every, rest


def gather_plan():
    size = {"A": A_ROWS * 512e-5, "B": (TOTAL - A_ROWS) * 512e-5}
    queue, busy, seen, count, order = [], {}, {}, 0, []

    def go(now, part, axis, d, k, other):
        nonlocal count
        length = size[part] * (0.5 if k == LAST[axis] else 1)
        begin = max(now, busy.get((axis, d), 0.0))
        busy[axis, d] = begin + length
        count += 1
        heapq.heappush(queue, (begin + length + 1.5, count, (part, axis, d, k, other)))

    for part, axis in FIRST:
        for d in range(2):
            go(0.0, part, axis, d, 1, 0)
    parts, packs = {}, []
    while queue:
        now, _, message = heapq.heappop(queue)
        while packs and packs[0][0] <= now:
            order.append(("pack", packs.pop(0)[1]))
        order.append(message)
        part, axis, d, k, other = message
        if k < LAST[axis]:
            go(now, part, axis, d, k + 1, other)
        key = (part, axis, k if k == LAST[axis] else message, other)
        seen[key] = seen.get(key, 0) + 1
        if k == LAST[axis] and seen[key] < 2:
            continue
        away = LAST[axis] if k == LAST[axis] else SIGN[d] * k
        turn = (part, axis) in (("A", "x"), ("B", "z"))
        if turn:
            for e in range(2):
                go(now, part, "z" if axis == "x" else "x", e, 1, away)
            order.append(("turn", part, away))
        row = other if axis == "x" else away
        if axis == "x" or part == "A":
            parts[part, row] = parts.get((part, row), 0) + 1
            if parts[part, row] == (3 if axis == "x" else 4):
                order.append(("sib", part, row))
                if parts.get(("B" if part == "A" else "A", row), 0) >= (3 if part == "B" and row == 0 else 4 if part == "B" else 3):
                    packs.append((now + 2.5, row))
    return order + [("pack", row) for _, row in packs]


def kernel(
    tok_ref,
    one_ref,
    two_ref,
    three_ref,
    gain_ref,
    scale_ref,
    wq_ref,
    wo_ref,
    every_ref,
    rest_ref,
    out_ref,
    gbuf,
    wd,
    wod,
    recv,
    res,
    pruned,
    picks,
    stage,
    small,
    normed,
    qkv,
    mixed,
    every,
    rest,
    tok_sem,
    table_sem,
    out_sem,
    za_send,
    za_recv,
    zb_send,
    zb_recv,
    xa_send,
    xa_recv,
    xb_send,
    xb_recv,
    sib_send,
    sib_recv,
    t_send,
    t_recv,
    ready,
    turn,
):
    micro, rows, feats = tok_ref.shape
    tiles = feats // LANE
    rows_in, rows_out = wq_ref.shape[0], wo_ref.shape[0]
    group_in, group_out = 8 * rows_in, 8 * rows_out
    width = 64 * rows_out
    heads = width // HDIM
    left = rows_in + rows_out - MAIN
    level = lax.axis_index("section")
    z = lax.axis_index("fsdp")
    dp = lax.axis_index("dp")
    x = dp // 2
    core = dp - 2 * x

    def zat(step):
        return lax.rem(z + step + 8, 8)

    def xat(step):
        return lax.rem(x + step + 4, 4)

    x_plus, x_minus = (level, z, xat(1) * 2 + core), (level, z, xat(-1) * 2 + core)
    z_plus, z_minus = (level, zat(1), dp), (level, zat(-1), dp)
    sibling = (level, z, x * 2 + 1 - core)
    y_plus, y_minus = (lax.rem(level + 1, 8), z, dp), (lax.rem(level + 7, 8), z, dp)

    barrier = pltpu.get_barrier_semaphore()
    partners = (x_plus, x_minus, z_plus, z_minus, sibling, y_plus, y_minus)
    for partner in partners:
        pl.semaphore_signal(barrier, inc=1, device_id=partner, device_id_type=MESH)

    stage[pl.ds(0, rows_in), :] = wq_ref[...].astype(jnp.float32)
    stage[pl.ds(rows_in, rows_out), :] = wo_ref[...].astype(jnp.float32)
    small[...] = jnp.zeros_like(small)
    for tile in range(tiles):
        lanes = slice(tile * LANE, (tile + 1) * LANE)
        gbuf[core, z, x, tile * MAIN : (tile + 1) * MAIN, :] = stage[0:MAIN, lanes].astype(jnp.bfloat16)
        small[tile * left : (tile + 1) * left, :] = stage[MAIN : MAIN + left, lanes]
    gbuf[core, z, x, tiles * MAIN : tiles * MAIN + REST, :] = small[...].astype(jnp.bfloat16)

    tables = (
        pltpu.make_async_copy(every_ref, every, table_sem.at[0]),
        pltpu.make_async_copy(rest_ref, rest, table_sem.at[1]),
    )
    for table in tables:
        table.start()
    pl.semaphore_wait(barrier, len(partners))

    total = tiles * MAIN + REST
    A, A1, A2 = pl.ds(0, A_ROWS), pl.ds(0, A_HALF), pl.ds(A_HALF, A_ROWS - A_HALF)
    B, B1, B2 = (
        pl.ds(A_ROWS, total - A_ROWS),
        pl.ds(A_ROWS, B_HALF),
        pl.ds(A_ROWS + B_HALF, total - A_ROWS - B_HALF),
    )

    started = []

    def send(part, ss, rs, to):
        copy = pltpu.make_async_remote_copy(
            src_ref=part, dst_ref=part, send_sem=ss, recv_sem=rs, device_id=to, device_id_type=MESH
        )
        copy.start()
        started.append(copy)

    def arrive(part, ss, rs):
        pltpu.make_async_remote_copy(
            src_ref=part, dst_ref=part, send_sem=ss, recv_sem=rs, device_id=z_plus, device_id_type=MESH
        ).wait_recv()

    targets = {"x": (x_plus, x_minus), "z": (z_plus, z_minus)}
    rows_of = {"A": (A, A1, A2), "B": (B, B1, B2)}

    def at(dz, dx, piece):
        return gbuf.at[core, zat(dz), xat(dx), piece]

    def lane_of(message):
        part, axis, d, k, other = message
        piece = rows_of[part][1 + d if k == LAST[axis] else 0]
        away = SIGN[d] * k
        place = at(other, away, piece) if axis == "x" else at(away, other, piece)
        if axis == "z" and part == "A":
            index = (d, k - 1, other % 4)
            return place, za_send.at[index], za_recv.at[index]
        if axis == "z":
            return place, zb_send.at[d, k - 1], zb_recv.at[d, k - 1]
        if part == "A":
            return place, xa_send.at[d, k - 1], xa_recv.at[d, k - 1]
        index = (other % 8, d, k - 1)
        return place, xb_send.at[index], xb_recv.at[index]

    def post(part, axis, d, k, other):
        piece = rows_of[part][1 + d if k == LAST[axis] else 0]
        away = SIGN[d] * (k - 1)
        place = at(other, away, piece) if axis == "x" else at(away, other, piece)
        _, ss, rs = lane_of((part, axis, d, k, other))
        send(place, ss, rs, targets[axis][d])

    def take(message):
        part, axis, d, k, other = message
        arrive(*lane_of(message))
        if k < LAST[axis]:
            post(part, axis, d, k + 1, other)

    def to_sibling(part, dz):
        i = (dz % 8, "AB".index(part))
        send(gbuf.at[core, zat(dz), :, rows_of[part][0]], sib_send.at[i], sib_recv.at[i], sibling)

    def pack(dz):
        g = zat(dz)
        for i, part in enumerate("AB"):
            index = (dz % 8, i)
            arrive(gbuf.at[1 - core, g, :, rows_of[part][0]], sib_send.at[index], sib_recv.at[index])
        tail = gbuf[:, g, :, tiles * MAIN : tiles * MAIN + REST, :].reshape(8 * REST, LANE)
        tail = jnp.dot(rest[...], tail, preferred_element_type=jnp.float32).astype(jnp.bfloat16)
        for tile in range(0, tiles, 2):
            count = min(2, tiles - tile)
            columns = [
                jnp.concatenate(
                    [
                        gbuf[:, g, :, t * MAIN : (t + 1) * MAIN, :].reshape(8 * MAIN, LANE),
                        tail[t * 8 * left : (t + 1) * 8 * left, :],
                    ],
                    axis=0,
                )
                for t in range(tile, tile + count)
            ]
            block = columns[0] if count == 1 else jnp.concatenate(columns, axis=1)
            dense = jnp.dot(every[...], block, preferred_element_type=jnp.float32).astype(jnp.bfloat16)
            lanes = slice(tile * LANE, (tile + count) * LANE)
            pad_in = wd.shape[1]
            wd[g, :, lanes] = dense[:pad_in]
            wod[g, :, lanes] = dense[pad_in:]

    for part, axis in FIRST:
        for d in range(2):
            post(part, axis, d, 1, 0)

    recv[...] = jnp.zeros_like(recv)

    @pl.when(level > 0)
    def _():
        pl.semaphore_signal(ready, inc=1, device_id=y_minus, device_id_type=MESH)

    @pl.when(level == 0)
    def _():
        pltpu.make_async_copy(tok_ref, recv, tok_sem).start()

    picks[...] = jnp.zeros_like(picks)
    for here, chosen in ((1, one_ref), (3, two_ref), (5, three_ref)):

        @pl.when(level == here)
        def _():
            count = chosen.shape[1]
            place = lax.broadcasted_iota(jnp.int32, (rows, count), 0)
            for m in range(micro):
                hit = place == chosen[m : m + 1, :]
                picks[m, :, 0:count] = jnp.where(hit, 1.0, 0.0).astype(jnp.bfloat16)

    for table in tables:
        table.wait()
    for event in gather_plan():
        if event[0] == "sib":
            to_sibling(*event[1:])
        elif event[0] == "pack":
            pack(event[1])
        elif event[0] == "turn":
            for d in range(2):
                post(event[1], "z" if event[1] == "A" else "x", d, 1, event[2])
        else:
            take(event)

    live = rows - 32 * (level >= 2).astype(jnp.int32)
    live = live - 32 * (level >= 4).astype(jnp.int32) - 16 * (level >= 6).astype(jnp.int32)

    def token_copy(m, source, count, low=0):
        i = 1 if low else 0
        return pltpu.make_async_remote_copy(
            src_ref=source.at[m, pl.ds(low, count)],
            dst_ref=recv.at[m, pl.ds(low, count)],
            send_sem=t_send.at[i, m],
            recv_sem=t_recv.at[i, m],
            device_id=y_plus,
            device_id_type=MESH,
        )

    @pl.when(level == 0)
    def _():
        pltpu.make_async_copy(tok_ref, recv, tok_sem).wait()

    counts = (one_ref.shape[1], two_ref.shape[1], three_ref.shape[1])
    incoming = ((2, 3, counts[0]), (4, 5, counts[1]), (6, 7, counts[2]))
    early = 3 * rows // 4

    def body(m, carry):
        @pl.when(level == 1)
        def _():
            token_copy(m, recv, early).wait_recv()
            token_copy(m, recv, rows - early, early).wait_recv()

        for low, high, count in incoming:

            @pl.when(jnp.logical_and(level >= low, level <= high))
            def _():
                token_copy(m, recv, count).wait_recv()

        values = recv[m].astype(jnp.float32)
        center = values - jnp.mean(values, axis=-1, keepdims=True)
        spread = jnp.mean(center * center, axis=-1, keepdims=True)
        normed[...] = (center * lax.rsqrt(spread + EPS) * gain_ref[...]).astype(jnp.bfloat16)

        every_row = wd.reshape(8 * wd.shape[1], feats)
        half = 4 * wd.shape[1]

        def project(i, carry):
            part = lax.dot_general(
                every_row[pl.ds(pl.multiple_of(i * half, 16), half), :],
                normed[...],
                (((1,), (1,)), ((), ())),
                preferred_element_type=jnp.float32,
            )
            for g in range(4):
                low = g * wd.shape[1]
                start = pl.multiple_of((i * 4 + g) * group_in, 8)
                qkv[pl.ds(start, group_in), :] = part[low : low + group_in]
            return carry

        lax.fori_loop(0, 2, project, 0)

        inside = lax.broadcasted_iota(jnp.int32, (rows, rows), 0) < live
        for h in range(heads):
            low = h * HDIM
            query = (qkv[low : low + HDIM, :].astype(jnp.bfloat16) * jnp.bfloat16(HDIM**-0.5))
            keys = qkv[width + low : width + low + HDIM, :].astype(jnp.bfloat16)
            vals = qkv[2 * width + low : 2 * width + low + HDIM, :].astype(jnp.bfloat16)
            scores = lax.dot_general(
                keys, query, (((0,), (0,)), ((), ())), preferred_element_type=jnp.float32
            )
            scores = jnp.where(inside, scores, -1e30)
            top = jnp.max(scores, axis=0, keepdims=True)
            expo = jnp.exp(scores - top)
            weights = (expo * (1.0 / jnp.sum(expo, axis=0, keepdims=True))).astype(jnp.bfloat16)
            mixed[low : low + HDIM, :] = jnp.dot(vals, weights, preferred_element_type=jnp.float32)

        parts = []
        gap = jnp.zeros((wod.shape[1] - group_out, rows), jnp.float32)
        for g in range(8):
            parts.append(mixed[g * group_out : (g + 1) * group_out, :])
            if gap.shape[0]:
                parts.append(gap)
        across = jnp.transpose(jnp.concatenate(parts, axis=0)).astype(jnp.bfloat16)
        alive = lax.broadcasted_iota(jnp.int32, (rows, LANE), 0) < live
        for low in range(0, feats, 4 * LANE):
            size = min(4 * LANE, feats - low)
            lanes = slice(low, low + size)
            block = wod[:, :, lanes].reshape(8 * wod.shape[1], size)
            branch = jnp.dot(across, block, preferred_element_type=jnp.float32)
            sums = recv[m, :, lanes].astype(jnp.float32) + scale_ref[:, lanes] * branch
            sums = jnp.where(alive[:, :1], sums, 0.0)
            res[m, :, lanes] = sums.astype(jnp.bfloat16)

        pltpu.make_async_copy(res.at[m], out_ref.at[m], out_sem.at[m]).start()

        @pl.when(jnp.logical_and(m == 0, level < 7))
        def _():
            pl.semaphore_wait(ready, 1)

        @pl.when(level == 0)
        def _():
            @pl.when(jnp.logical_or(m > 0, core == 1))
            def _():
                pl.semaphore_wait(turn, 1)

            token_copy(m, res, early).start()
            token_copy(m, res, rows - early, early).start()
            token_copy(m, res, early).wait_send()

            @pl.when(jnp.logical_or(m < micro - 1, core == 0))
            def _():
                pl.semaphore_signal(turn, inc=1, device_id=sibling, device_id_type=MESH)

        for here, count in ((2, counts[0]), (4, counts[1]), (6, counts[2])):

            @pl.when(level == here)
            def _():
                token_copy(m, res, count).start()

        @pl.when(jnp.logical_and(lax.rem(level, 2) == 1, level < 7))
        def _():
            for low in range(0, feats, 4 * LANE):
                size = min(4 * LANE, feats - low)
                lanes = slice(low, low + size)
                taken = lax.dot_general(
                    picks[m], res[m, :, lanes], (((0,), (0,)), ((), ())), preferred_element_type=jnp.float32
                )
                pruned[m, :, lanes] = taken.astype(jnp.bfloat16)

        for here, count in ((1, counts[0]), (3, counts[1]), (5, counts[2])):

            @pl.when(level == here)
            def _():
                token_copy(m, pruned, count).start()

        return carry

    lax.fori_loop(0, micro, body, 0)

    for copy in started:
        copy.wait_send()

    def finish(m, carry):
        pltpu.make_async_copy(res.at[m], out_ref.at[m], out_sem.at[m]).wait()
        @pl.when(level == 0)
        def _():
            token_copy(m, res, rows - early, early).wait_send()

        for here, count in ((2, counts[0]), (4, counts[1]), (6, counts[2])):

            @pl.when(level == here)
            def _():
                token_copy(m, res, count).wait_send()

        for here, count in ((1, counts[0]), (3, counts[1]), (5, counts[2])):

            @pl.when(level == here)
            def _():
                token_copy(m, pruned, count).wait_send()

        return carry

    lax.fori_loop(0, micro, finish, 0)


def shards(tokens_in, keep_one, keep_two, keep_three, norm_gain, layer_scale, w_qkv, w_out):
    micro, _, rows, feats = tokens_in.shape
    rows_in, rows_out = w_qkv.shape[1], w_out.shape[1]
    tiles = feats // LANE
    every, rest = compaction(rows_in, rows_out, tiles)
    pad_in = -(-8 * rows_in // 16) * 16
    pad_out = -(-8 * rows_out // 16) * 16
    vmem = pl.BlockSpec(memory_space=pltpu.VMEM)
    dma = pltpu.SemaphoreType.DMA
    stash = pl.pallas_call(
        kernel,
        out_shape=jax.ShapeDtypeStruct((micro, rows, feats), jnp.bfloat16),
        in_specs=[pl.BlockSpec(memory_space=pl.ANY)] + [vmem] * 7 + [pl.BlockSpec(memory_space=pl.ANY)] * 2,
        out_specs=pl.BlockSpec(memory_space=pl.ANY),
        scratch_shapes=[
            pltpu.VMEM((2, 8, 4, tiles * MAIN + REST, LANE), jnp.bfloat16),
            pltpu.VMEM((8, pad_in, feats), jnp.bfloat16),
            pltpu.VMEM((8, pad_out, feats), jnp.bfloat16),
            pltpu.VMEM((micro, rows, feats), jnp.bfloat16),
            pltpu.VMEM((micro, rows, feats), jnp.bfloat16),
            pltpu.VMEM((micro, rows, feats), jnp.bfloat16),
            pltpu.VMEM((micro, rows, rows), jnp.bfloat16),
            pltpu.VMEM((64, feats), jnp.float32),
            pltpu.VMEM((REST, LANE), jnp.float32),
            pltpu.VMEM((rows, feats), jnp.bfloat16),
            pltpu.VMEM((64 * rows_in, rows), jnp.float32),
            pltpu.VMEM((64 * rows_out, rows), jnp.float32),
            pltpu.VMEM(every.shape, jnp.bfloat16),
            pltpu.VMEM(rest.shape, jnp.bfloat16),
            dma,
            dma((2,)),
            dma((micro,)),
            dma((2, 4, 4)),
            dma((2, 4, 4)),
            dma((2, 4)),
            dma((2, 4)),
            dma((2, 2)),
            dma((2, 2)),
            dma((8, 2, 2)),
            dma((8, 2, 2)),
            dma((8, 2)),
            dma((8, 2)),
            dma((2, micro)),
            dma((2, micro)),
            pltpu.SemaphoreType.REGULAR,
            pltpu.SemaphoreType.REGULAR,
        ],
        compiler_params=pltpu.CompilerParams(
            collective_id=0, has_side_effects=True, vmem_limit_bytes=60 * 1024 * 1024
        ),
    )(
        tokens_in[:, 0],
        keep_one[:, 0],
        keep_two[:, 0],
        keep_three[:, 0],
        norm_gain,
        layer_scale,
        w_qkv[0],
        w_out[0],
        jnp.asarray(every, jnp.bfloat16),
        jnp.asarray(rest, jnp.bfloat16),
    )
    return stash[None, :, None]


def solution(mesh):
    return jax.shard_map(
        shards,
        mesh=mesh,
        in_specs=(
            P(None, ("fsdp", "dp"), None, None),
            P(None, ("fsdp", "dp"), None),
            P(None, ("fsdp", "dp"), None),
            P(None, ("fsdp", "dp"), None),
            P("section", None),
            P("section", None),
            P("section", ("fsdp", "dp"), None),
            P("section", ("fsdp", "dp"), None),
        ),
        out_specs=P("section", None, ("fsdp", "dp"), None, None),
        check_vma=False,
    )
```

```python
import heapq

import jax
import jax.numpy as jnp
import numpy as np
from jax import lax
from jax.experimental import pallas as pl
from jax.experimental.pallas import tpu as pltpu
from jax.sharding import PartitionSpec as P

MESH = pl.DeviceIdType.MESH
HDIM = 64
EPS = 1e-06
LANE = 128
MAIN = 48
REST = 64
A_ROWS = 272
A_HALF = 144
B_HALF = 208
TOTAL = 13 * MAIN + REST
LAST = {"x": 2, "z": 4}
SIGN = (-1, 1)
CUTS = (0, 768, 1280, 1664)
FIRST = (("B", "z"), ("A", "x"), ("A", "z"), ("B", "x"))


def compaction(rows_in, rows_out, tiles):
    pad_in = -(-8 * rows_in // 16) * 16
    pad_out = -(-8 * rows_out // 16) * 16
    first = MAIN - rows_in
    left = rows_out - first
    every = np.zeros((pad_in + pad_out, 8 * MAIN + 8 * left), np.float32)
    rest = np.zeros((tiles * 8 * left, 8 * REST), np.float32)
    for core in range(2):
        for x in range(4):
            place, rank = core * 4 + x, x * 2 + core
            for i in range(rows_in):
                every[rank * rows_in + i, place * MAIN + i] = 1
            for i in range(first):
                every[pad_in + rank * rows_out + i, place * MAIN + rows_in + i] = 1
            for i in range(left):
                every[pad_in + rank * rows_out + first + i, 8 * MAIN + place * left + i] = 1
                for tile in range(tiles):
                    rest[tile * 8 * left + place * left + i, place * REST + tile * left + i] = 1
    return every, rest


def gather_plan():
    size = {"A": A_ROWS * 512e-5, "B": (TOTAL - A_ROWS) * 512e-5}
    queue, busy, seen, count, order = [], {}, {}, 0, []

    def go(now, part, axis, d, k, other):
        nonlocal count
        length = size[part] * (0.5 if k == LAST[axis] else 1)
        begin = max(now, busy.get((axis, d), 0.0))
        busy[axis, d] = begin + length
        count += 1
        heapq.heappush(queue, (begin + length + 1.5, count, (part, axis, d, k, other)))

    for part, axis in FIRST:
        for d in range(2):
            go(0.0, part, axis, d, 1, 0)
    parts, packs = {}, []
    while queue:
        now, _, message = heapq.heappop(queue)
        while packs and packs[0][0] <= now:
            order.append(("pack", packs.pop(0)[1]))
        order.append(message)
        part, axis, d, k, other = message
        if k < LAST[axis]:
            go(now, part, axis, d, k + 1, other)
        key = (part, axis, k if k == LAST[axis] else message, other)
        seen[key] = seen.get(key, 0) + 1
        if k == LAST[axis] and seen[key] < 2:
            continue
        away = LAST[axis] if k == LAST[axis] else SIGN[d] * k
        turn = (part, axis) in (("A", "x"), ("B", "z"))
        if turn:
            for e in range(2):
                go(now, part, "z" if axis == "x" else "x", e, 1, away)
            order.append(("turn", part, away))
        row = other if axis == "x" else away
        if axis == "x" or part == "A":
            parts[part, row] = parts.get((part, row), 0) + 1
            if parts[part, row] == (3 if axis == "x" else 4):
                order.append(("sib", part, row))
                if parts.get(("B" if part == "A" else "A", row), 0) >= (3 if part == "B" and row == 0 else 4 if part == "B" else 3):
                    packs.append((now + 2.5, row))
    return order + [("pack", row) for _, row in packs]


def kernel(
    tok_ref,
    one_ref,
    two_ref,
    three_ref,
    gain_ref,
    scale_ref,
    wq_ref,
    wo_ref,
    every_ref,
    rest_ref,
    out_ref,
    gbuf,
    wd,
    wod,
    recv,
    res,
    pruned,
    picks,
    stage,
    small,
    normed,
    qkv,
    mixed,
    every,
    rest,
    partial,
    stat_in,
    stat_out,
    tok_sem,
    table_sem,
    out_sem,
    za_send,
    za_recv,
    zb_send,
    zb_recv,
    xa_send,
    xa_recv,
    xb_send,
    xb_recv,
    sib_send,
    sib_recv,
    t_send,
    t_recv,
    ready,
    turn,
):
    micro, rows, feats = tok_ref.shape
    tiles = feats // LANE
    rows_in, rows_out = wq_ref.shape[0], wo_ref.shape[0]
    group_in, group_out = 8 * rows_in, 8 * rows_out
    width = 64 * rows_out
    heads = width // HDIM
    left = rows_in + rows_out - MAIN
    level = lax.axis_index("section")
    z = lax.axis_index("fsdp")
    dp = lax.axis_index("dp")
    x = dp // 2
    core = dp - 2 * x

    def zat(step):
        return lax.rem(z + step + 8, 8)

    def xat(step):
        return lax.rem(x + step + 4, 4)

    x_plus, x_minus = (level, z, xat(1) * 2 + core), (level, z, xat(-1) * 2 + core)
    z_plus, z_minus = (level, zat(1), dp), (level, zat(-1), dp)
    sibling = (level, z, x * 2 + 1 - core)
    y_plus, y_minus = (lax.rem(level + 1, 8), z, dp), (lax.rem(level + 7, 8), z, dp)

    barrier = pltpu.get_barrier_semaphore()
    partners = (x_plus, x_minus, z_plus, z_minus, sibling, y_plus, y_minus)
    for partner in partners:
        pl.semaphore_signal(barrier, inc=1, device_id=partner, device_id_type=MESH)

    stage[pl.ds(0, rows_in), :] = wq_ref[...].astype(jnp.float32)
    stage[pl.ds(rows_in, rows_out), :] = wo_ref[...].astype(jnp.float32)
    small[...] = jnp.zeros_like(small)
    for tile in range(tiles):
        lanes = slice(tile * LANE, (tile + 1) * LANE)
        gbuf[core, z, x, tile * MAIN : (tile + 1) * MAIN, :] = stage[0:MAIN, lanes].astype(jnp.bfloat16)
        small[tile * left : (tile + 1) * left, :] = stage[MAIN : MAIN + left, lanes]
    gbuf[core, z, x, tiles * MAIN : tiles * MAIN + REST, :] = small[...].astype(jnp.bfloat16)

    tables = (
        pltpu.make_async_copy(every_ref, every, table_sem.at[0]),
        pltpu.make_async_copy(rest_ref, rest, table_sem.at[1]),
    )
    for table in tables:
        table.start()
    pl.semaphore_wait(barrier, len(partners))

    total = tiles * MAIN + REST
    A, A1, A2 = pl.ds(0, A_ROWS), pl.ds(0, A_HALF), pl.ds(A_HALF, A_ROWS - A_HALF)
    B, B1, B2 = (
        pl.ds(A_ROWS, total - A_ROWS),
        pl.ds(A_ROWS, B_HALF),
        pl.ds(A_ROWS + B_HALF, total - A_ROWS - B_HALF),
    )

    started = []

    def send(part, ss, rs, to):
        copy = pltpu.make_async_remote_copy(
            src_ref=part, dst_ref=part, send_sem=ss, recv_sem=rs, device_id=to, device_id_type=MESH
        )
        copy.start()
        started.append(copy)

    def arrive(part, ss, rs):
        pltpu.make_async_remote_copy(
            src_ref=part, dst_ref=part, send_sem=ss, recv_sem=rs, device_id=z_plus, device_id_type=MESH
        ).wait_recv()

    targets = {"x": (x_plus, x_minus), "z": (z_plus, z_minus)}
    rows_of = {"A": (A, A1, A2), "B": (B, B1, B2)}

    def at(dz, dx, piece):
        return gbuf.at[core, zat(dz), xat(dx), piece]

    def lane_of(message):
        part, axis, d, k, other = message
        piece = rows_of[part][1 + d if k == LAST[axis] else 0]
        away = SIGN[d] * k
        place = at(other, away, piece) if axis == "x" else at(away, other, piece)
        if axis == "z" and part == "A":
            index = (d, k - 1, other % 4)
            return place, za_send.at[index], za_recv.at[index]
        if axis == "z":
            return place, zb_send.at[d, k - 1], zb_recv.at[d, k - 1]
        if part == "A":
            return place, xa_send.at[d, k - 1], xa_recv.at[d, k - 1]
        index = (other % 8, d, k - 1)
        return place, xb_send.at[index], xb_recv.at[index]

    def post(part, axis, d, k, other):
        piece = rows_of[part][1 + d if k == LAST[axis] else 0]
        away = SIGN[d] * (k - 1)
        place = at(other, away, piece) if axis == "x" else at(away, other, piece)
        _, ss, rs = lane_of((part, axis, d, k, other))
        send(place, ss, rs, targets[axis][d])

    def take(message):
        part, axis, d, k, other = message
        arrive(*lane_of(message))
        if k < LAST[axis]:
            post(part, axis, d, k + 1, other)

    def to_sibling(part, dz):
        i = (dz % 8, "AB".index(part))
        send(gbuf.at[core, zat(dz), :, rows_of[part][0]], sib_send.at[i], sib_recv.at[i], sibling)

    def pack(dz):
        g = zat(dz)
        for i, part in enumerate("AB"):
            index = (dz % 8, i)
            arrive(gbuf.at[1 - core, g, :, rows_of[part][0]], sib_send.at[index], sib_recv.at[index])
        tail = gbuf[:, g, :, tiles * MAIN : tiles * MAIN + REST, :].reshape(8 * REST, LANE)
        tail = jnp.dot(rest[...], tail, preferred_element_type=jnp.float32).astype(jnp.bfloat16)
        for tile in range(0, tiles, 2):
            count = min(2, tiles - tile)
            columns = [
                jnp.concatenate(
                    [
                        gbuf[:, g, :, t * MAIN : (t + 1) * MAIN, :].reshape(8 * MAIN, LANE),
                        tail[t * 8 * left : (t + 1) * 8 * left, :],
                    ],
                    axis=0,
                )
                for t in range(tile, tile + count)
            ]
            block = columns[0] if count == 1 else jnp.concatenate(columns, axis=1)
            dense = jnp.dot(every[...], block, preferred_element_type=jnp.float32).astype(jnp.bfloat16)
            lanes = slice(tile * LANE, (tile + count) * LANE)
            pad_in = wd.shape[1]
            wd[g, :, lanes] = dense[:pad_in]
            wod[g, :, lanes] = dense[pad_in:]

    for part, axis in FIRST:
        for d in range(2):
            post(part, axis, d, 1, 0)

    recv[...] = jnp.zeros_like(recv)

    @pl.when(level > 0)
    def _():
        pl.semaphore_signal(ready, inc=1, device_id=y_minus, device_id_type=MESH)

    @pl.when(level == 0)
    def _():
        pltpu.make_async_copy(tok_ref, recv, tok_sem).start()

    picks[...] = jnp.zeros_like(picks)
    for here, chosen in ((1, one_ref), (3, two_ref), (5, three_ref)):

        @pl.when(level == here)
        def _():
            count = chosen.shape[1]
            place = lax.broadcasted_iota(jnp.int32, (rows, count), 0)
            for m in range(micro):
                hit = place == chosen[m : m + 1, :]
                picks[m, :, 0:count] = jnp.where(hit, 1.0, 0.0).astype(jnp.bfloat16)

    for table in tables:
        table.wait()
    for event in gather_plan():
        if event[0] == "sib":
            to_sibling(*event[1:])
        elif event[0] == "pack":
            pack(event[1])
        elif event[0] == "turn":
            for d in range(2):
                post(event[1], "z" if event[1] == "A" else "x", d, 1, event[2])
        else:
            take(event)

    live = rows - 32 * (level >= 2).astype(jnp.int32)
    live = live - 32 * (level >= 4).astype(jnp.int32) - 16 * (level >= 6).astype(jnp.int32)

    def token_copy(i, m, source, count):
        if i == 3:
            src, dst = stat_out.at[m], stat_in.at[m]
        else:
            lanes = pl.ds(CUTS[i], CUTS[i + 1] - CUTS[i])
            src, dst = source.at[m, pl.ds(0, count), lanes], recv.at[m, pl.ds(0, count), lanes]
        return pltpu.make_async_remote_copy(
            src_ref=src,
            dst_ref=dst,
            send_sem=t_send.at[i, m],
            recv_sem=t_recv.at[i, m],
            device_id=y_plus,
            device_id_type=MESH,
        )

    def row_stats(values):
        values = values.astype(jnp.float32)
        mean = jnp.mean(values, axis=-1, keepdims=True)
        center = values - mean
        spread = lax.rsqrt(jnp.mean(center * center, axis=-1, keepdims=True) + EPS)
        column = lax.broadcasted_iota(jnp.int32, (rows, LANE), 1)
        both = jnp.where(column == 0, mean, jnp.where(column == 1, spread, 0.0))
        return jnp.transpose(both)[:8]

    @pl.when(level == 0)
    def _():
        pltpu.make_async_copy(tok_ref, recv, tok_sem).wait()

        def prepare(m, carry):
            stat_in[m] = row_stats(recv[m])
            return carry

        lax.fori_loop(0, micro, prepare, 0)

    counts = (one_ref.shape[1], two_ref.shape[1], three_ref.shape[1])
    incoming = ((1, 1, rows), (2, 3, counts[0]), (4, 5, counts[1]), (6, 7, counts[2]))
    outgoing = ((2, res, counts[0]), (4, res, counts[1]), (6, res, counts[2]))
    outgoing += ((1, pruned, counts[0]), (3, pruned, counts[1]), (5, pruned, counts[2]))
    order = (3, 0, 1, 2)

    def body(m, carry):
        def await_tokens(i):
            for low, high, count in incoming:

                @pl.when(jnp.logical_and(level >= low, level <= high))
                def _():
                    token_copy(i, m, recv, count).wait_recv()

        await_tokens(3)
        columns = jnp.transpose(jnp.concatenate([stat_in[m], jnp.zeros((LANE - 8, rows), jnp.float32)], axis=0))
        mean, spread = columns[:, 0:1], columns[:, 1:2]
        every_row = wd.reshape(8 * wd.shape[1], feats)
        half = 4 * wd.shape[1]
        for i in range(3):
            lanes = slice(CUTS[i], CUTS[i + 1])
            await_tokens(i)
            center = recv[m, :, lanes].astype(jnp.float32) - mean
            normed[:, lanes] = (center * spread * gain_ref[:, lanes]).astype(jnp.bfloat16)

            def project(j, carry):
                these = pl.ds(pl.multiple_of(j * half, 16), half)
                part = lax.dot_general(
                    every_row[these, lanes],
                    normed[:, lanes],
                    (((1,), (1,)), ((), ())),
                    preferred_element_type=jnp.float32,
                )
                if i > 0:
                    part = part + partial[these, :]
                if i < 2:
                    partial[these, :] = part
                else:
                    for g in range(4):
                        low = g * wd.shape[1]
                        start = pl.multiple_of((j * 4 + g) * group_in, 8)
                        qkv[pl.ds(start, group_in), :] = part[low : low + group_in]
                return carry

            lax.fori_loop(0, 2, project, 0)

        inside = lax.broadcasted_iota(jnp.int32, (rows, rows), 0) < live
        for h in range(heads):
            low = h * HDIM
            query = (qkv[low : low + HDIM, :].astype(jnp.bfloat16) * jnp.bfloat16(HDIM**-0.5))
            keys = qkv[width + low : width + low + HDIM, :].astype(jnp.bfloat16)
            vals = qkv[2 * width + low : 2 * width + low + HDIM, :].astype(jnp.bfloat16)
            scores = lax.dot_general(
                keys, query, (((0,), (0,)), ((), ())), preferred_element_type=jnp.float32
            )
            scores = jnp.where(inside, scores, -1e30)
            top = jnp.max(scores, axis=0, keepdims=True)
            expo = jnp.exp(scores - top)
            weights = (expo * (1.0 / jnp.sum(expo, axis=0, keepdims=True))).astype(jnp.bfloat16)
            mixed[low : low + HDIM, :] = jnp.dot(vals, weights, preferred_element_type=jnp.float32)

        parts = []
        gap = jnp.zeros((wod.shape[1] - group_out, rows), jnp.float32)
        for g in range(8):
            parts.append(mixed[g * group_out : (g + 1) * group_out, :])
            if gap.shape[0]:
                parts.append(gap)
        across = jnp.transpose(jnp.concatenate(parts, axis=0)).astype(jnp.bfloat16)
        alive = lax.broadcasted_iota(jnp.int32, (rows, LANE), 0) < live
        for low in range(0, feats, 4 * LANE):
            size = min(4 * LANE, feats - low)
            lanes = slice(low, low + size)
            block = wod[:, :, lanes].reshape(8 * wod.shape[1], size)
            branch = jnp.dot(across, block, preferred_element_type=jnp.float32)
            sums = recv[m, :, lanes].astype(jnp.float32) + scale_ref[:, lanes] * branch
            sums = jnp.where(alive[:, :1], sums, 0.0)
            res[m, :, lanes] = sums.astype(jnp.bfloat16)

        pltpu.make_async_copy(res.at[m], out_ref.at[m], out_sem.at[m]).start()

        @pl.when(jnp.logical_and(m == 0, level < 7))
        def _():
            pl.semaphore_wait(ready, 1)

        @pl.when(lax.rem(level, 2) == 0)
        def _():
            stat_out[m] = row_stats(res[m])

        @pl.when(level == 0)
        def _():
            @pl.when(jnp.logical_or(m > 0, core == 1))
            def _():
                pl.semaphore_wait(turn, 1)

            for i in order:
                token_copy(i, m, res, rows).start()
            token_copy(1, m, res, rows).wait_send()

            @pl.when(jnp.logical_or(m < micro - 1, core == 0))
            def _():
                pl.semaphore_signal(turn, inc=1, device_id=sibling, device_id_type=MESH)

        @pl.when(jnp.logical_and(lax.rem(level, 2) == 1, level < 7))
        def _():
            for low in range(0, feats, 4 * LANE):
                size = min(4 * LANE, feats - low)
                lanes = slice(low, low + size)
                taken = lax.dot_general(
                    picks[m], res[m, :, lanes], (((0,), (0,)), ((), ())), preferred_element_type=jnp.float32
                )
                pruned[m, :, lanes] = taken.astype(jnp.bfloat16)
            stat_out[m] = row_stats(pruned[m])

        for here, source, count in outgoing:

            @pl.when(level == here)
            def _():
                for i in order:
                    token_copy(i, m, source, count).start()

        return carry

    lax.fori_loop(0, micro, body, 0)

    for copy in started:
        copy.wait_send()

    def finish(m, carry):
        pltpu.make_async_copy(res.at[m], out_ref.at[m], out_sem.at[m]).wait()
        @pl.when(level == 0)
        def _():
            for i in (3, 0, 2):
                token_copy(i, m, res, rows).wait_send()

        for here, source, count in outgoing:

            @pl.when(level == here)
            def _():
                for i in order:
                    token_copy(i, m, source, count).wait_send()

        return carry

    lax.fori_loop(0, micro, finish, 0)


def shards(tokens_in, keep_one, keep_two, keep_three, norm_gain, layer_scale, w_qkv, w_out):
    micro, _, rows, feats = tokens_in.shape
    rows_in, rows_out = w_qkv.shape[1], w_out.shape[1]
    tiles = feats // LANE
    every, rest = compaction(rows_in, rows_out, tiles)
    pad_in = -(-8 * rows_in // 16) * 16
    pad_out = -(-8 * rows_out // 16) * 16
    vmem = pl.BlockSpec(memory_space=pltpu.VMEM)
    dma = pltpu.SemaphoreType.DMA
    stash = pl.pallas_call(
        kernel,
        out_shape=jax.ShapeDtypeStruct((micro, rows, feats), jnp.bfloat16),
        in_specs=[pl.BlockSpec(memory_space=pl.ANY)] + [vmem] * 7 + [pl.BlockSpec(memory_space=pl.ANY)] * 2,
        out_specs=pl.BlockSpec(memory_space=pl.ANY),
        scratch_shapes=[
            pltpu.VMEM((2, 8, 4, tiles * MAIN + REST, LANE), jnp.bfloat16),
            pltpu.VMEM((8, pad_in, feats), jnp.bfloat16),
            pltpu.VMEM((8, pad_out, feats), jnp.bfloat16),
            pltpu.VMEM((micro, rows, feats), jnp.bfloat16),
            pltpu.VMEM((micro, rows, feats), jnp.bfloat16),
            pltpu.VMEM((micro, rows, feats), jnp.bfloat16),
            pltpu.VMEM((micro, rows, rows), jnp.bfloat16),
            pltpu.VMEM((64, feats), jnp.float32),
            pltpu.VMEM((REST, LANE), jnp.float32),
            pltpu.VMEM((rows, feats), jnp.bfloat16),
            pltpu.VMEM((64 * rows_in, rows), jnp.float32),
            pltpu.VMEM((64 * rows_out, rows), jnp.float32),
            pltpu.VMEM(every.shape, jnp.bfloat16),
            pltpu.VMEM(rest.shape, jnp.bfloat16),
            pltpu.VMEM((8 * pad_in, rows), jnp.float32),
            pltpu.VMEM((micro, 8, rows), jnp.float32),
            pltpu.VMEM((micro, 8, rows), jnp.float32),
            dma,
            dma((2,)),
            dma((micro,)),
            dma((2, 4, 4)),
            dma((2, 4, 4)),
            dma((2, 4)),
            dma((2, 4)),
            dma((2, 2)),
            dma((2, 2)),
            dma((8, 2, 2)),
            dma((8, 2, 2)),
            dma((8, 2)),
            dma((8, 2)),
            dma((4, micro)),
            dma((4, micro)),
            pltpu.SemaphoreType.REGULAR,
            pltpu.SemaphoreType.REGULAR,
        ],
        compiler_params=pltpu.CompilerParams(
            collective_id=0, has_side_effects=True, vmem_limit_bytes=60 * 1024 * 1024
        ),
    )(
        tokens_in[:, 0],
        keep_one[:, 0],
        keep_two[:, 0],
        keep_three[:, 0],
        norm_gain,
        layer_scale,
        w_qkv[0],
        w_out[0],
        jnp.asarray(every, jnp.bfloat16),
        jnp.asarray(rest, jnp.bfloat16),
    )
    return stash[None, :, None]


def solution(mesh):
    return jax.shard_map(
        shards,
        mesh=mesh,
        in_specs=(
            P(None, ("fsdp", "dp"), None, None),
            P(None, ("fsdp", "dp"), None),
            P(None, ("fsdp", "dp"), None),
            P(None, ("fsdp", "dp"), None),
            P("section", None),
            P("section", None),
            P("section", ("fsdp", "dp"), None),
            P("section", ("fsdp", "dp"), None),
        ),
        out_specs=P("section", None, ("fsdp", "dp"), None, None),
        check_vma=False,
    )
```

```python
import heapq

import jax
import jax.numpy as jnp
import numpy as np
from jax import lax
from jax.experimental import pallas as pl
from jax.experimental.pallas import tpu as pltpu
from jax.sharding import PartitionSpec as P

MESH = pl.DeviceIdType.MESH
HDIM = 64
EPS = 1e-06
LANE = 128
MAIN = 48
REST = 64
A_ROWS = 272
A_HALF = 144
B_HALF = 208
TOTAL = 13 * MAIN + REST
LAST = {"x": 2, "z": 4}
SIGN = (-1, 1)
CUTS = (0, 768, 1280, 1664)
AHEAD = 1
FIRST = (("B", "z"), ("A", "x"), ("A", "z"), ("B", "x"))


def compaction(rows_in, rows_out, tiles):
    pad_in = -(-8 * rows_in // 16) * 16
    pad_out = -(-8 * rows_out // 16) * 16
    first = MAIN - rows_in
    left = rows_out - first
    every = np.zeros((pad_in + pad_out, 8 * MAIN + 8 * left), np.float32)
    rest = np.zeros((tiles * 8 * left, 8 * REST), np.float32)
    for core in range(2):
        for x in range(4):
            place, rank = core * 4 + x, x * 2 + core
            for i in range(rows_in):
                every[rank * rows_in + i, place * MAIN + i] = 1
            for i in range(first):
                every[pad_in + rank * rows_out + i, place * MAIN + rows_in + i] = 1
            for i in range(left):
                every[pad_in + rank * rows_out + first + i, 8 * MAIN + place * left + i] = 1
                for tile in range(tiles):
                    rest[tile * 8 * left + place * left + i, place * REST + tile * left + i] = 1
    return every, rest


def gather_plan():
    size = {"A": A_ROWS * 512e-5, "B": (TOTAL - A_ROWS) * 512e-5}
    queue, busy, seen, count, order = [], {}, {}, 0, []

    def go(now, part, axis, d, k, other):
        nonlocal count
        length = size[part] * (0.5 if k == LAST[axis] else 1)
        begin = max(now, busy.get((axis, d), 0.0))
        busy[axis, d] = begin + length
        count += 1
        heapq.heappush(queue, (begin + length + 1.5, count, (part, axis, d, k, other)))

    for part, axis in FIRST:
        for d in range(2):
            go(0.0, part, axis, d, 1, 0)
    parts, packs = {}, []
    while queue:
        now, _, message = heapq.heappop(queue)
        while packs and packs[0][0] <= now:
            order.append(("pack", packs.pop(0)[1]))
        order.append(message)
        part, axis, d, k, other = message
        if k < LAST[axis]:
            go(now, part, axis, d, k + 1, other)
        key = (part, axis, k if k == LAST[axis] else message, other)
        seen[key] = seen.get(key, 0) + 1
        if k == LAST[axis] and seen[key] < 2:
            continue
        away = LAST[axis] if k == LAST[axis] else SIGN[d] * k
        turn = (part, axis) in (("A", "x"), ("B", "z"))
        if turn:
            for e in range(2):
                go(now, part, "z" if axis == "x" else "x", e, 1, away)
            order.append(("turn", part, away))
        row = other if axis == "x" else away
        if axis == "x" or part == "A":
            parts[part, row] = parts.get((part, row), 0) + 1
            if parts[part, row] == (3 if axis == "x" else 4):
                order.append(("sib", part, row))
                if parts.get(("B" if part == "A" else "A", row), 0) >= (3 if part == "B" and row == 0 else 4 if part == "B" else 3):
                    packs.append((now + 2.5, row))
    return order + [("pack", row) for _, row in packs]


def kernel(
    tok_ref,
    one_ref,
    two_ref,
    three_ref,
    gain_ref,
    scale_ref,
    wq_ref,
    wo_ref,
    every_ref,
    rest_ref,
    out_ref,
    gbuf,
    wd,
    wod,
    recv,
    res,
    pruned,
    picks,
    stage,
    small,
    normed,
    ahead,
    qkv,
    mixed,
    every,
    rest,
    partial,
    stat_in,
    stat_out,
    tok_sem,
    table_sem,
    out_sem,
    za_send,
    za_recv,
    zb_send,
    zb_recv,
    xa_send,
    xa_recv,
    xb_send,
    xb_recv,
    sib_send,
    sib_recv,
    t_send,
    t_recv,
    ready,
    turn,
):
    micro, rows, feats = tok_ref.shape
    tiles = feats // LANE
    rows_in, rows_out = wq_ref.shape[0], wo_ref.shape[0]
    group_in, group_out = 8 * rows_in, 8 * rows_out
    width = 64 * rows_out
    heads = width // HDIM
    left = rows_in + rows_out - MAIN
    level = lax.axis_index("section")
    z = lax.axis_index("fsdp")
    dp = lax.axis_index("dp")
    x = dp // 2
    core = dp - 2 * x

    def zat(step):
        return lax.rem(z + step + 8, 8)

    def xat(step):
        return lax.rem(x + step + 4, 4)

    x_plus, x_minus = (level, z, xat(1) * 2 + core), (level, z, xat(-1) * 2 + core)
    z_plus, z_minus = (level, zat(1), dp), (level, zat(-1), dp)
    sibling = (level, z, x * 2 + 1 - core)
    y_plus, y_minus = (lax.rem(level + 1, 8), z, dp), (lax.rem(level + 7, 8), z, dp)

    barrier = pltpu.get_barrier_semaphore()
    partners = (x_plus, x_minus, z_plus, z_minus, sibling, y_plus, y_minus)
    for partner in partners:
        pl.semaphore_signal(barrier, inc=1, device_id=partner, device_id_type=MESH)

    stage[pl.ds(0, rows_in), :] = wq_ref[...].astype(jnp.float32)
    stage[pl.ds(rows_in, rows_out), :] = wo_ref[...].astype(jnp.float32)
    small[...] = jnp.zeros_like(small)
    for tile in range(tiles):
        lanes = slice(tile * LANE, (tile + 1) * LANE)
        gbuf[core, z, x, tile * MAIN : (tile + 1) * MAIN, :] = stage[0:MAIN, lanes].astype(jnp.bfloat16)
        small[tile * left : (tile + 1) * left, :] = stage[MAIN : MAIN + left, lanes]
    gbuf[core, z, x, tiles * MAIN : tiles * MAIN + REST, :] = small[...].astype(jnp.bfloat16)

    tables = (
        pltpu.make_async_copy(every_ref, every, table_sem.at[0]),
        pltpu.make_async_copy(rest_ref, rest, table_sem.at[1]),
    )
    for table in tables:
        table.start()
    pl.semaphore_wait(barrier, len(partners))

    total = tiles * MAIN + REST
    A, A1, A2 = pl.ds(0, A_ROWS), pl.ds(0, A_HALF), pl.ds(A_HALF, A_ROWS - A_HALF)
    B, B1, B2 = (
        pl.ds(A_ROWS, total - A_ROWS),
        pl.ds(A_ROWS, B_HALF),
        pl.ds(A_ROWS + B_HALF, total - A_ROWS - B_HALF),
    )

    started = []

    def send(part, ss, rs, to):
        copy = pltpu.make_async_remote_copy(
            src_ref=part, dst_ref=part, send_sem=ss, recv_sem=rs, device_id=to, device_id_type=MESH
        )
        copy.start()
        started.append(copy)

    def arrive(part, ss, rs):
        pltpu.make_async_remote_copy(
            src_ref=part, dst_ref=part, send_sem=ss, recv_sem=rs, device_id=z_plus, device_id_type=MESH
        ).wait_recv()

    targets = {"x": (x_plus, x_minus), "z": (z_plus, z_minus)}
    rows_of = {"A": (A, A1, A2), "B": (B, B1, B2)}

    def at(dz, dx, piece):
        return gbuf.at[core, zat(dz), xat(dx), piece]

    def lane_of(message):
        part, axis, d, k, other = message
        piece = rows_of[part][1 + d if k == LAST[axis] else 0]
        away = SIGN[d] * k
        place = at(other, away, piece) if axis == "x" else at(away, other, piece)
        if axis == "z" and part == "A":
            index = (d, k - 1, other % 4)
            return place, za_send.at[index], za_recv.at[index]
        if axis == "z":
            return place, zb_send.at[d, k - 1], zb_recv.at[d, k - 1]
        if part == "A":
            return place, xa_send.at[d, k - 1], xa_recv.at[d, k - 1]
        index = (other % 8, d, k - 1)
        return place, xb_send.at[index], xb_recv.at[index]

    def post(part, axis, d, k, other):
        piece = rows_of[part][1 + d if k == LAST[axis] else 0]
        away = SIGN[d] * (k - 1)
        place = at(other, away, piece) if axis == "x" else at(away, other, piece)
        _, ss, rs = lane_of((part, axis, d, k, other))
        send(place, ss, rs, targets[axis][d])

    def take(message):
        part, axis, d, k, other = message
        arrive(*lane_of(message))
        if k < LAST[axis]:
            post(part, axis, d, k + 1, other)

    def to_sibling(part, dz):
        i = (dz % 8, "AB".index(part))
        send(gbuf.at[core, zat(dz), :, rows_of[part][0]], sib_send.at[i], sib_recv.at[i], sibling)

    def pack(dz):
        g = zat(dz)
        for i, part in enumerate("AB"):
            index = (dz % 8, i)
            arrive(gbuf.at[1 - core, g, :, rows_of[part][0]], sib_send.at[index], sib_recv.at[index])
        tail = gbuf[:, g, :, tiles * MAIN : tiles * MAIN + REST, :].reshape(8 * REST, LANE)
        tail = jnp.dot(rest[...], tail, preferred_element_type=jnp.float32).astype(jnp.bfloat16)
        for tile in range(0, tiles, 2):
            count = min(2, tiles - tile)
            columns = [
                jnp.concatenate(
                    [
                        gbuf[:, g, :, t * MAIN : (t + 1) * MAIN, :].reshape(8 * MAIN, LANE),
                        tail[t * 8 * left : (t + 1) * 8 * left, :],
                    ],
                    axis=0,
                )
                for t in range(tile, tile + count)
            ]
            block = columns[0] if count == 1 else jnp.concatenate(columns, axis=1)
            dense = jnp.dot(every[...], block, preferred_element_type=jnp.float32).astype(jnp.bfloat16)
            lanes = slice(tile * LANE, (tile + count) * LANE)
            pad_in = wd.shape[1]
            wd[g, :, lanes] = dense[:pad_in]
            wod[g, :, lanes] = dense[pad_in:]

        @pl.when(level == 0)
        def _():
            part = lax.dot_general(
                wd[g], ahead[...], (((1,), (1,)), ((), ())), preferred_element_type=jnp.float32
            )
            start = pl.multiple_of(g * group_in, 8)
            for m in range(AHEAD):
                qkv[m, pl.ds(start, group_in), :] = part[:group_in, m * rows : (m + 1) * rows]

    for part, axis in FIRST:
        for d in range(2):
            post(part, axis, d, 1, 0)

    recv[...] = jnp.zeros_like(recv)

    @pl.when(level > 0)
    def _():
        pl.semaphore_signal(ready, inc=1, device_id=y_minus, device_id_type=MESH)

    @pl.when(level == 0)
    def _():
        pltpu.make_async_copy(tok_ref, recv, tok_sem).start()

    picks[...] = jnp.zeros_like(picks)
    for here, chosen in ((1, one_ref), (3, two_ref), (5, three_ref)):

        @pl.when(level == here)
        def _():
            count = chosen.shape[1]
            place = lax.broadcasted_iota(jnp.int32, (rows, count), 0)
            for m in range(micro):
                hit = place == chosen[m : m + 1, :]
                picks[m, :, 0:count] = jnp.where(hit, 1.0, 0.0).astype(jnp.bfloat16)

    def norm_ahead():
        @pl.when(level == 0)
        def _():
            pltpu.make_async_copy(tok_ref, recv, tok_sem).wait()

            def norm(m, carry):
                values = recv[m].astype(jnp.float32)
                center = values - jnp.mean(values, axis=-1, keepdims=True)
                spread = lax.rsqrt(jnp.mean(center * center, axis=-1, keepdims=True) + EPS)
                result = (center * spread * gain_ref[...]).astype(jnp.bfloat16)
                ahead[pl.ds(pl.multiple_of(m * rows, rows), rows), :] = result
                return carry

            lax.fori_loop(0, AHEAD, norm, 0)

    for table in tables:
        table.wait()
    plan = gather_plan()
    first_pack = [event[0] for event in plan].index("pack")
    for i, event in enumerate(plan):
        if i == first_pack:
            norm_ahead()
        if event[0] == "sib":
            to_sibling(*event[1:])
        elif event[0] == "pack":
            pack(event[1])
        elif event[0] == "turn":
            for d in range(2):
                post(event[1], "z" if event[1] == "A" else "x", d, 1, event[2])
        else:
            take(event)

    live = rows - 32 * (level >= 2).astype(jnp.int32)
    live = live - 32 * (level >= 4).astype(jnp.int32) - 16 * (level >= 6).astype(jnp.int32)

    def token_copy(i, m, source, count):
        if i == 3:
            src, dst = stat_out.at[m], stat_in.at[m]
        else:
            lanes = pl.ds(CUTS[i], CUTS[i + 1] - CUTS[i])
            src, dst = source.at[m, pl.ds(0, count), lanes], recv.at[m, pl.ds(0, count), lanes]
        return pltpu.make_async_remote_copy(
            src_ref=src,
            dst_ref=dst,
            send_sem=t_send.at[i, m],
            recv_sem=t_recv.at[i, m],
            device_id=y_plus,
            device_id_type=MESH,
        )

    def row_stats(values):
        values = values.astype(jnp.float32)
        mean = jnp.mean(values, axis=-1, keepdims=True)
        center = values - mean
        spread = lax.rsqrt(jnp.mean(center * center, axis=-1, keepdims=True) + EPS)
        column = lax.broadcasted_iota(jnp.int32, (rows, LANE), 1)
        both = jnp.where(column == 0, mean, jnp.where(column == 1, spread, 0.0))
        return jnp.transpose(both)[:8]

    counts = (one_ref.shape[1], two_ref.shape[1], three_ref.shape[1])
    incoming = ((1, 1, rows), (2, 3, counts[0]), (4, 5, counts[1]), (6, 7, counts[2]))
    outgoing = ((2, res, counts[0]), (4, res, counts[1]), (6, res, counts[2]))
    outgoing += ((1, pruned, counts[0]), (3, pruned, counts[1]), (5, pruned, counts[2]))
    order = (3, 0, 1, 2)

    def body(m, carry):
        slot = lax.rem(m, AHEAD)
        def await_tokens(i):
            for low, high, count in incoming:

                @pl.when(jnp.logical_and(level >= low, level <= high))
                def _():
                    token_copy(i, m, recv, count).wait_recv()

        @pl.when(jnp.logical_and(m == 0, level < 7))
        def _():
            pl.semaphore_wait(ready, 1)

        @pl.when(jnp.logical_or(level > 0, m >= AHEAD))
        def _():
            @pl.when(jnp.logical_and(level == 0, m >= AHEAD))
            def _():
                stat_in[m] = row_stats(recv[m])

            await_tokens(3)
            columns = jnp.transpose(jnp.concatenate([stat_in[m], jnp.zeros((LANE - 8, rows), jnp.float32)], axis=0))
            mean, spread = columns[:, 0:1], columns[:, 1:2]
            every_row = wd.reshape(8 * wd.shape[1], feats)
            half = 4 * wd.shape[1]
            for i in range(3):
                lanes = slice(CUTS[i], CUTS[i + 1])
                await_tokens(i)
                center = recv[m, :, lanes].astype(jnp.float32) - mean
                normed[:, lanes] = (center * spread * gain_ref[:, lanes]).astype(jnp.bfloat16)

                def project(j, carry):
                    these = pl.ds(pl.multiple_of(j * half, 16), half)
                    part = lax.dot_general(
                        every_row[these, lanes],
                        normed[:, lanes],
                        (((1,), (1,)), ((), ())),
                        preferred_element_type=jnp.float32,
                    )
                    if i > 0:
                        part = part + partial[these, :]
                    if i < 2:
                        partial[these, :] = part
                    else:
                        for g in range(4):
                            low = g * wd.shape[1]
                            start = pl.multiple_of((j * 4 + g) * group_in, 8)
                            qkv[slot, pl.ds(start, group_in), :] = part[low : low + group_in]
                    return carry

                lax.fori_loop(0, 2, project, 0)

        @pl.when(jnp.logical_and(level == 0, m > 0))
        def _():
            token_copy(1, m - 1, res, rows).wait_send()
            pl.semaphore_signal(turn, inc=1, device_id=sibling, device_id_type=MESH)

        inside = lax.broadcasted_iota(jnp.int32, (rows, rows), 0) < live
        for h in range(heads):
            low = h * HDIM
            query = (qkv[slot, low : low + HDIM, :].astype(jnp.bfloat16) * jnp.bfloat16(HDIM**-0.5))
            keys = qkv[slot, width + low : width + low + HDIM, :].astype(jnp.bfloat16)
            vals = qkv[slot, 2 * width + low : 2 * width + low + HDIM, :].astype(jnp.bfloat16)
            scores = lax.dot_general(
                keys, query, (((0,), (0,)), ((), ())), preferred_element_type=jnp.float32
            )
            scores = jnp.where(inside, scores, -1e30)
            top = jnp.max(scores, axis=0, keepdims=True)
            expo = jnp.exp(scores - top)
            weights = (expo * (1.0 / jnp.sum(expo, axis=0, keepdims=True))).astype(jnp.bfloat16)
            mixed[low : low + HDIM, :] = jnp.dot(vals, weights, preferred_element_type=jnp.float32)

        parts = []
        gap = jnp.zeros((wod.shape[1] - group_out, rows), jnp.float32)
        for g in range(8):
            parts.append(mixed[g * group_out : (g + 1) * group_out, :])
            if gap.shape[0]:
                parts.append(gap)
        across = jnp.transpose(jnp.concatenate(parts, axis=0)).astype(jnp.bfloat16)
        alive = lax.broadcasted_iota(jnp.int32, (rows, LANE), 0) < live
        prunes = jnp.logical_and(lax.rem(level, 2) == 1, level < 7)

        def start(which):
            for here, source, count in outgoing:

                @pl.when(level == here)
                def _():
                    for i in which:
                        token_copy(i, m, source, count).start()

        for i in range(3):
            lanes = slice(CUTS[i], CUTS[i + 1])
            block = wod[:, :, lanes].reshape(8 * wod.shape[1], CUTS[i + 1] - CUTS[i])
            branch = jnp.dot(across, block, preferred_element_type=jnp.float32)
            sums = recv[m, :, lanes].astype(jnp.float32) + scale_ref[:, lanes] * branch
            sums = jnp.where(alive[:, :1], sums, 0.0)
            res[m, :, lanes] = sums.astype(jnp.bfloat16)

            @pl.when(prunes)
            def _():
                taken = lax.dot_general(
                    picks[m], res[m, :, lanes], (((0,), (0,)), ((), ())), preferred_element_type=jnp.float32
                )
                pruned[m, :, lanes] = taken.astype(jnp.bfloat16)

            if i == 0:
                start((0,))

        @pl.when(prunes)
        def _():
            stat_out[m] = row_stats(pruned[m])

        @pl.when(lax.rem(level, 2) == 0)
        def _():
            stat_out[m] = row_stats(res[m])

        start((3, 1, 2))
        pltpu.make_async_copy(res.at[m], out_ref.at[m], out_sem.at[m]).start()

        @pl.when(level == 0)
        def _():
            @pl.when(jnp.logical_or(m > 0, core == 1))
            def _():
                pl.semaphore_wait(turn, 1)

            for i in order:
                token_copy(i, m, res, rows).start()

            @pl.when(jnp.logical_and(m == micro - 1, core == 0))
            def _():
                token_copy(1, m, res, rows).wait_send()
                pl.semaphore_signal(turn, inc=1, device_id=sibling, device_id_type=MESH)

        return carry

    lax.fori_loop(0, micro, body, 0)

    for copy in started:
        copy.wait_send()

    def finish(m, carry):
        pltpu.make_async_copy(res.at[m], out_ref.at[m], out_sem.at[m]).wait()
        @pl.when(level == 0)
        def _():
            for i in (3, 0, 2):
                token_copy(i, m, res, rows).wait_send()

            @pl.when(jnp.logical_and(m == micro - 1, core == 1))
            def _():
                token_copy(1, m, res, rows).wait_send()

        for here, source, count in outgoing:

            @pl.when(level == here)
            def _():
                for i in order:
                    token_copy(i, m, source, count).wait_send()

        return carry

    lax.fori_loop(0, micro, finish, 0)


def shards(tokens_in, keep_one, keep_two, keep_three, norm_gain, layer_scale, w_qkv, w_out):
    micro, _, rows, feats = tokens_in.shape
    rows_in, rows_out = w_qkv.shape[1], w_out.shape[1]
    tiles = feats // LANE
    every, rest = compaction(rows_in, rows_out, tiles)
    pad_in = -(-8 * rows_in // 16) * 16
    pad_out = -(-8 * rows_out // 16) * 16
    vmem = pl.BlockSpec(memory_space=pltpu.VMEM)
    dma = pltpu.SemaphoreType.DMA
    stash = pl.pallas_call(
        kernel,
        out_shape=jax.ShapeDtypeStruct((micro, rows, feats), jnp.bfloat16),
        in_specs=[pl.BlockSpec(memory_space=pl.ANY)] + [vmem] * 7 + [pl.BlockSpec(memory_space=pl.ANY)] * 2,
        out_specs=pl.BlockSpec(memory_space=pl.ANY),
        scratch_shapes=[
            pltpu.VMEM((2, 8, 4, tiles * MAIN + REST, LANE), jnp.bfloat16),
            pltpu.VMEM((8, pad_in, feats), jnp.bfloat16),
            pltpu.VMEM((8, pad_out, feats), jnp.bfloat16),
            pltpu.VMEM((micro, rows, feats), jnp.bfloat16),
            pltpu.VMEM((micro, rows, feats), jnp.bfloat16),
            pltpu.VMEM((micro, rows, feats), jnp.bfloat16),
            pltpu.VMEM((micro, rows, rows), jnp.bfloat16),
            pltpu.VMEM((64, feats), jnp.float32),
            pltpu.VMEM((REST, LANE), jnp.float32),
            pltpu.VMEM((rows, feats), jnp.bfloat16),
            pltpu.VMEM((AHEAD * rows, feats), jnp.bfloat16),
            pltpu.VMEM((AHEAD, 64 * rows_in, rows), jnp.float32),
            pltpu.VMEM((64 * rows_out, rows), jnp.float32),
            pltpu.VMEM(every.shape, jnp.bfloat16),
            pltpu.VMEM(rest.shape, jnp.bfloat16),
            pltpu.VMEM((8 * pad_in, rows), jnp.float32),
            pltpu.VMEM((micro, 8, rows), jnp.float32),
            pltpu.VMEM((micro, 8, rows), jnp.float32),
            dma,
            dma((2,)),
            dma((micro,)),
            dma((2, 4, 4)),
            dma((2, 4, 4)),
            dma((2, 4)),
            dma((2, 4)),
            dma((2, 2)),
            dma((2, 2)),
            dma((8, 2, 2)),
            dma((8, 2, 2)),
            dma((8, 2)),
            dma((8, 2)),
            dma((4, micro)),
            dma((4, micro)),
            pltpu.SemaphoreType.REGULAR,
            pltpu.SemaphoreType.REGULAR,
        ],
        compiler_params=pltpu.CompilerParams(
            collective_id=0, has_side_effects=True, vmem_limit_bytes=60 * 1024 * 1024
        ),
    )(
        tokens_in[:, 0],
        keep_one[:, 0],
        keep_two[:, 0],
        keep_three[:, 0],
        norm_gain,
        layer_scale,
        w_qkv[0],
        w_out[0],
        jnp.asarray(every, jnp.bfloat16),
        jnp.asarray(rest, jnp.bfloat16),
    )
    return stash[None, :, None]


def solution(mesh):
    return jax.shard_map(
        shards,
        mesh=mesh,
        in_specs=(
            P(None, ("fsdp", "dp"), None, None),
            P(None, ("fsdp", "dp"), None),
            P(None, ("fsdp", "dp"), None),
            P(None, ("fsdp", "dp"), None),
            P("section", None),
            P("section", None),
            P("section", ("fsdp", "dp"), None),
            P("section", ("fsdp", "dp"), None),
        ),
        out_specs=P("section", None, ("fsdp", "dp"), None, None),
        check_vma=False,
    )
```

```python
import heapq

import jax
import jax.numpy as jnp
import numpy as np
from jax import lax
from jax.experimental import pallas as pl
from jax.experimental.pallas import tpu as pltpu
from jax.sharding import PartitionSpec as P

MESH = pl.DeviceIdType.MESH
HDIM = 64
EPS = 1e-06
LANE = 128
MAIN = 48
REST = 64
A_ROWS = 240
A_HALF = 128
B_HALF = 224
TOTAL = 13 * MAIN + REST
LAST = {"x": 2, "z": 4}
SIGN = (-1, 1)
CUTS = (0, 768, 1280, 1664)
AHEAD = 1
FIRST = (("B", "z"), ("A", "x"), ("A", "z"), ("B", "x"))


def compaction(rows_in, rows_out, tiles):
    pad_in = -(-8 * rows_in // 16) * 16
    pad_out = -(-8 * rows_out // 16) * 16
    first = MAIN - rows_in
    left = rows_out - first
    every = np.zeros((pad_in + pad_out, 8 * MAIN + 8 * left), np.float32)
    rest = np.zeros((tiles * 8 * left, 8 * REST), np.float32)
    for core in range(2):
        for x in range(4):
            place, rank = core * 4 + x, x * 2 + core
            for i in range(rows_in):
                every[rank * rows_in + i, place * MAIN + i] = 1
            for i in range(first):
                every[pad_in + rank * rows_out + i, place * MAIN + rows_in + i] = 1
            for i in range(left):
                every[pad_in + rank * rows_out + first + i, 8 * MAIN + place * left + i] = 1
                for tile in range(tiles):
                    rest[tile * 8 * left + place * left + i, place * REST + tile * left + i] = 1
    return every, rest


def gather_plan():
    size = {"A": A_ROWS * 512e-5, "B": (TOTAL - A_ROWS) * 512e-5}
    queue, busy, seen, count, order = [], {}, {}, 0, []

    def go(now, part, axis, d, k, other):
        nonlocal count
        length = size[part] * (0.5 if k == LAST[axis] else 1)
        begin = max(now, busy.get((axis, d), 0.0))
        busy[axis, d] = begin + length
        count += 1
        heapq.heappush(queue, (begin + length + 1.5, count, (part, axis, d, k, other)))

    for part, axis in FIRST:
        for d in range(2):
            go(0.0, part, axis, d, 1, 0)
    parts, packs = {}, []
    while queue:
        now, _, message = heapq.heappop(queue)
        while packs and packs[0][0] <= now:
            order.append(("pack", packs.pop(0)[1]))
        order.append(message)
        part, axis, d, k, other = message
        if k < LAST[axis]:
            go(now, part, axis, d, k + 1, other)
        key = (part, axis, k if k == LAST[axis] else message, other)
        seen[key] = seen.get(key, 0) + 1
        if k == LAST[axis] and seen[key] < 2:
            continue
        away = LAST[axis] if k == LAST[axis] else SIGN[d] * k
        turn = (part, axis) in (("A", "x"), ("B", "z"))
        if turn:
            for e in range(2):
                go(now, part, "z" if axis == "x" else "x", e, 1, away)
            order.append(("turn", part, away))
        row = other if axis == "x" else away
        if axis == "x" or part == "A":
            parts[part, row] = parts.get((part, row), 0) + 1
            if parts[part, row] == (3 if axis == "x" else 4):
                order.append(("sib", part, row))
                if parts.get(("B" if part == "A" else "A", row), 0) >= (3 if part == "B" and row == 0 else 4 if part == "B" else 3):
                    packs.append((now + 2.5, row))
    return order + [("pack", row) for _, row in packs]


def kernel(
    tok_ref,
    one_ref,
    two_ref,
    three_ref,
    gain_ref,
    scale_ref,
    wq_ref,
    wo_ref,
    every_ref,
    rest_ref,
    out_ref,
    gbuf,
    wd,
    wod,
    recv,
    res,
    pruned,
    picks,
    stage,
    small,
    normed,
    ahead,
    qkv,
    mixed,
    every,
    rest,
    partial,
    stat_in,
    stat_out,
    tok_sem,
    table_sem,
    out_sem,
    za_send,
    za_recv,
    zb_send,
    zb_recv,
    xa_send,
    xa_recv,
    xb_send,
    xb_recv,
    sib_send,
    sib_recv,
    t_send,
    t_recv,
    ready,
    turn,
):
    micro, rows, feats = tok_ref.shape
    tiles = feats // LANE
    rows_in, rows_out = wq_ref.shape[0], wo_ref.shape[0]
    group_in, group_out = 8 * rows_in, 8 * rows_out
    width = 64 * rows_out
    heads = width // HDIM
    left = rows_in + rows_out - MAIN
    level = lax.axis_index("section")
    z = lax.axis_index("fsdp")
    dp = lax.axis_index("dp")
    x = dp // 2
    core = dp - 2 * x

    def zat(step):
        return lax.rem(z + step + 8, 8)

    def xat(step):
        return lax.rem(x + step + 4, 4)

    x_plus, x_minus = (level, z, xat(1) * 2 + core), (level, z, xat(-1) * 2 + core)
    z_plus, z_minus = (level, zat(1), dp), (level, zat(-1), dp)
    sibling = (level, z, x * 2 + 1 - core)
    y_plus, y_minus = (lax.rem(level + 1, 8), z, dp), (lax.rem(level + 7, 8), z, dp)

    barrier = pltpu.get_barrier_semaphore()
    partners = (x_plus, x_minus, z_plus, z_minus, sibling, y_plus, y_minus)
    for partner in partners:
        pl.semaphore_signal(barrier, inc=1, device_id=partner, device_id_type=MESH)

    stage[pl.ds(0, rows_in), :] = wq_ref[...].astype(jnp.float32)
    stage[pl.ds(rows_in, rows_out), :] = wo_ref[...].astype(jnp.float32)
    small[...] = jnp.zeros_like(small)
    for tile in range(tiles):
        lanes = slice(tile * LANE, (tile + 1) * LANE)
        gbuf[core, z, x, tile * MAIN : (tile + 1) * MAIN, :] = stage[0:MAIN, lanes].astype(jnp.bfloat16)
        small[tile * left : (tile + 1) * left, :] = stage[MAIN : MAIN + left, lanes]
    gbuf[core, z, x, tiles * MAIN : tiles * MAIN + REST, :] = small[...].astype(jnp.bfloat16)

    tables = (
        pltpu.make_async_copy(every_ref, every, table_sem.at[0]),
        pltpu.make_async_copy(rest_ref, rest, table_sem.at[1]),
    )
    for table in tables:
        table.start()
    pl.semaphore_wait(barrier, len(partners))

    total = tiles * MAIN + REST
    A, A1, A2 = pl.ds(0, A_ROWS), pl.ds(0, A_HALF), pl.ds(A_HALF, A_ROWS - A_HALF)
    B, B1, B2 = (
        pl.ds(A_ROWS, total - A_ROWS),
        pl.ds(A_ROWS, B_HALF),
        pl.ds(A_ROWS + B_HALF, total - A_ROWS - B_HALF),
    )

    started = []

    def send(part, ss, rs, to):
        copy = pltpu.make_async_remote_copy(
            src_ref=part, dst_ref=part, send_sem=ss, recv_sem=rs, device_id=to, device_id_type=MESH
        )
        copy.start()
        started.append(copy)

    def arrive(part, ss, rs):
        pltpu.make_async_remote_copy(
            src_ref=part, dst_ref=part, send_sem=ss, recv_sem=rs, device_id=z_plus, device_id_type=MESH
        ).wait_recv()

    targets = {"x": (x_plus, x_minus), "z": (z_plus, z_minus)}
    rows_of = {"A": (A, A1, A2), "B": (B, B1, B2)}

    def at(dz, dx, piece):
        return gbuf.at[core, zat(dz), xat(dx), piece]

    def lane_of(message):
        part, axis, d, k, other = message
        piece = rows_of[part][1 + d if k == LAST[axis] else 0]
        away = SIGN[d] * k
        place = at(other, away, piece) if axis == "x" else at(away, other, piece)
        if axis == "z" and part == "A":
            index = (d, k - 1, other % 4)
            return place, za_send.at[index], za_recv.at[index]
        if axis == "z":
            return place, zb_send.at[d, k - 1], zb_recv.at[d, k - 1]
        if part == "A":
            return place, xa_send.at[d, k - 1], xa_recv.at[d, k - 1]
        index = (other % 8, d, k - 1)
        return place, xb_send.at[index], xb_recv.at[index]

    def post(part, axis, d, k, other):
        piece = rows_of[part][1 + d if k == LAST[axis] else 0]
        away = SIGN[d] * (k - 1)
        place = at(other, away, piece) if axis == "x" else at(away, other, piece)
        _, ss, rs = lane_of((part, axis, d, k, other))
        send(place, ss, rs, targets[axis][d])

    def take(message):
        part, axis, d, k, other = message
        arrive(*lane_of(message))
        if k < LAST[axis]:
            post(part, axis, d, k + 1, other)

    def to_sibling(part, dz):
        i = (dz % 8, "AB".index(part))
        send(gbuf.at[core, zat(dz), :, rows_of[part][0]], sib_send.at[i], sib_recv.at[i], sibling)

    def pack(dz):
        g = zat(dz)
        for i, part in enumerate("AB"):
            index = (dz % 8, i)
            arrive(gbuf.at[1 - core, g, :, rows_of[part][0]], sib_send.at[index], sib_recv.at[index])
        tail = gbuf[:, g, :, tiles * MAIN : tiles * MAIN + REST, :].reshape(8 * REST, LANE)
        tail = jnp.dot(rest[...], tail, preferred_element_type=jnp.float32).astype(jnp.bfloat16)
        for tile in range(0, tiles, 2):
            count = min(2, tiles - tile)
            columns = [
                jnp.concatenate(
                    [
                        gbuf[:, g, :, t * MAIN : (t + 1) * MAIN, :].reshape(8 * MAIN, LANE),
                        tail[t * 8 * left : (t + 1) * 8 * left, :],
                    ],
                    axis=0,
                )
                for t in range(tile, tile + count)
            ]
            block = columns[0] if count == 1 else jnp.concatenate(columns, axis=1)
            dense = jnp.dot(every[...], block, preferred_element_type=jnp.float32).astype(jnp.bfloat16)
            lanes = slice(tile * LANE, (tile + count) * LANE)
            pad_in = wd.shape[1]
            wd[g, :, lanes] = dense[:pad_in]
            wod[g, :, lanes] = dense[pad_in:]

        @pl.when(level == 0)
        def _():
            part = lax.dot_general(
                wd[g], ahead[...], (((1,), (1,)), ((), ())), preferred_element_type=jnp.float32
            )
            start = pl.multiple_of(g * group_in, 8)
            for m in range(AHEAD):
                qkv[m, pl.ds(start, group_in), :] = part[:group_in, m * rows : (m + 1) * rows]

    for part, axis in FIRST:
        for d in range(2):
            post(part, axis, d, 1, 0)

    recv[...] = jnp.zeros_like(recv)

    @pl.when(level > 0)
    def _():
        pl.semaphore_signal(ready, inc=1, device_id=y_minus, device_id_type=MESH)

    @pl.when(level == 0)
    def _():
        pltpu.make_async_copy(tok_ref, recv, tok_sem).start()

    picks[...] = jnp.zeros_like(picks)
    for here, chosen in ((1, one_ref), (3, two_ref), (5, three_ref)):

        @pl.when(level == here)
        def _():
            count = chosen.shape[1]
            place = lax.broadcasted_iota(jnp.int32, (rows, count), 0)
            for m in range(micro):
                hit = place == chosen[m : m + 1, :]
                picks[m, :, 0:count] = jnp.where(hit, 1.0, 0.0).astype(jnp.bfloat16)

    def norm_ahead():
        @pl.when(level == 0)
        def _():
            pltpu.make_async_copy(tok_ref, recv, tok_sem).wait()

            def norm(m, carry):
                values = recv[m].astype(jnp.float32)
                center = values - jnp.mean(values, axis=-1, keepdims=True)
                spread = lax.rsqrt(jnp.mean(center * center, axis=-1, keepdims=True) + EPS)
                result = (center * spread * gain_ref[...]).astype(jnp.bfloat16)
                ahead[pl.ds(pl.multiple_of(m * rows, rows), rows), :] = result
                return carry

            lax.fori_loop(0, AHEAD, norm, 0)

    for table in tables:
        table.wait()
    plan = gather_plan()
    first_pack = [event[0] for event in plan].index("pack")
    for i, event in enumerate(plan):
        if i == first_pack:
            norm_ahead()
        if event[0] == "sib":
            to_sibling(*event[1:])
        elif event[0] == "pack":
            pack(event[1])
        elif event[0] == "turn":
            for d in range(2):
                post(event[1], "z" if event[1] == "A" else "x", d, 1, event[2])
        else:
            take(event)

    live = rows - 32 * (level >= 2).astype(jnp.int32)
    live = live - 32 * (level >= 4).astype(jnp.int32) - 16 * (level >= 6).astype(jnp.int32)

    def token_copy(i, m, source, count):
        if i == 3:
            src, dst = stat_out.at[m], stat_in.at[m]
        else:
            lanes = pl.ds(CUTS[i], CUTS[i + 1] - CUTS[i])
            src, dst = source.at[m, pl.ds(0, count), lanes], recv.at[m, pl.ds(0, count), lanes]
        return pltpu.make_async_remote_copy(
            src_ref=src,
            dst_ref=dst,
            send_sem=t_send.at[i, m],
            recv_sem=t_recv.at[i, m],
            device_id=y_plus,
            device_id_type=MESH,
        )

    def row_stats(values):
        values = values.astype(jnp.float32)
        mean = jnp.mean(values, axis=-1, keepdims=True)
        center = values - mean
        spread = lax.rsqrt(jnp.mean(center * center, axis=-1, keepdims=True) + EPS)
        column = lax.broadcasted_iota(jnp.int32, (rows, LANE), 1)
        both = jnp.where(column == 0, mean, jnp.where(column == 1, spread, 0.0))
        return jnp.transpose(both)[:8]

    counts = (one_ref.shape[1], two_ref.shape[1], three_ref.shape[1])
    incoming = ((1, 1, rows), (2, 3, counts[0]), (4, 5, counts[1]), (6, 7, counts[2]))
    outgoing = ((2, res, counts[0]), (4, res, counts[1]), (6, res, counts[2]))
    outgoing += ((1, pruned, counts[0]), (3, pruned, counts[1]), (5, pruned, counts[2]))
    order = (3, 0, 1, 2)

    def body(m, carry):
        slot = lax.rem(m, AHEAD)
        def await_tokens(i):
            for low, high, count in incoming:

                @pl.when(jnp.logical_and(level >= low, level <= high))
                def _():
                    token_copy(i, m, recv, count).wait_recv()

        @pl.when(jnp.logical_and(m == 0, level < 7))
        def _():
            pl.semaphore_wait(ready, 1)

        @pl.when(jnp.logical_or(level > 0, m >= AHEAD))
        def _():
            @pl.when(jnp.logical_and(level == 0, m >= AHEAD))
            def _():
                stat_in[m] = row_stats(recv[m])

            await_tokens(3)
            columns = jnp.transpose(jnp.concatenate([stat_in[m], jnp.zeros((LANE - 8, rows), jnp.float32)], axis=0))
            mean, spread = columns[:, 0:1], columns[:, 1:2]
            every_row = wd.reshape(8 * wd.shape[1], feats)
            half = 4 * wd.shape[1]
            for i in range(3):
                lanes = slice(CUTS[i], CUTS[i + 1])
                await_tokens(i)
                center = recv[m, :, lanes].astype(jnp.float32) - mean
                normed[:, lanes] = (center * spread * gain_ref[:, lanes]).astype(jnp.bfloat16)

                def project(j, carry):
                    these = pl.ds(pl.multiple_of(j * half, 16), half)
                    part = lax.dot_general(
                        every_row[these, lanes],
                        normed[:, lanes],
                        (((1,), (1,)), ((), ())),
                        preferred_element_type=jnp.float32,
                    )
                    if i > 0:
                        part = part + partial[these, :]
                    if i < 2:
                        partial[these, :] = part
                    else:
                        for g in range(4):
                            low = g * wd.shape[1]
                            start = pl.multiple_of((j * 4 + g) * group_in, 8)
                            qkv[slot, pl.ds(start, group_in), :] = part[low : low + group_in]
                    return carry

                lax.fori_loop(0, 2, project, 0)

        @pl.when(jnp.logical_and(level == 0, m > 0))
        def _():
            token_copy(1, m - 1, res, rows).wait_send()
            pl.semaphore_signal(turn, inc=1, device_id=sibling, device_id_type=MESH)

        inside = lax.broadcasted_iota(jnp.int32, (rows, rows), 0) < live
        for h in range(heads):
            low = h * HDIM
            query = (qkv[slot, low : low + HDIM, :].astype(jnp.bfloat16) * jnp.bfloat16(HDIM**-0.5))
            keys = qkv[slot, width + low : width + low + HDIM, :].astype(jnp.bfloat16)
            vals = qkv[slot, 2 * width + low : 2 * width + low + HDIM, :].astype(jnp.bfloat16)
            scores = lax.dot_general(
                keys, query, (((0,), (0,)), ((), ())), preferred_element_type=jnp.float32
            )
            scores = jnp.where(inside, scores, -1e30)
            top = jnp.max(scores, axis=0, keepdims=True)
            expo = jnp.exp(scores - top)
            weights = (expo * (1.0 / jnp.sum(expo, axis=0, keepdims=True))).astype(jnp.bfloat16)
            mixed[low : low + HDIM, :] = jnp.dot(vals, weights, preferred_element_type=jnp.float32)

        parts = []
        gap = jnp.zeros((wod.shape[1] - group_out, rows), jnp.float32)
        for g in range(8):
            parts.append(mixed[g * group_out : (g + 1) * group_out, :])
            if gap.shape[0]:
                parts.append(gap)
        across = jnp.transpose(jnp.concatenate(parts, axis=0)).astype(jnp.bfloat16)
        alive = lax.broadcasted_iota(jnp.int32, (rows, LANE), 0) < live
        prunes = jnp.logical_and(lax.rem(level, 2) == 1, level < 7)

        def start(which):
            for here, source, count in outgoing:

                @pl.when(level == here)
                def _():
                    for i in which:
                        token_copy(i, m, source, count).start()

        for i in range(3):
            lanes = slice(CUTS[i], CUTS[i + 1])
            block = wod[:, :, lanes].reshape(8 * wod.shape[1], CUTS[i + 1] - CUTS[i])
            branch = jnp.dot(across, block, preferred_element_type=jnp.float32)
            sums = recv[m, :, lanes].astype(jnp.float32) + scale_ref[:, lanes] * branch
            sums = jnp.where(alive[:, :1], sums, 0.0)
            res[m, :, lanes] = sums.astype(jnp.bfloat16)

            @pl.when(prunes)
            def _():
                taken = lax.dot_general(
                    picks[m], res[m, :, lanes], (((0,), (0,)), ((), ())), preferred_element_type=jnp.float32
                )
                pruned[m, :, lanes] = taken.astype(jnp.bfloat16)

            if i == 0:
                start((0,))

        @pl.when(prunes)
        def _():
            stat_out[m] = row_stats(pruned[m])

        @pl.when(lax.rem(level, 2) == 0)
        def _():
            stat_out[m] = row_stats(res[m])

        start((3, 1, 2))
        pltpu.make_async_copy(res.at[m], out_ref.at[m], out_sem.at[m]).start()

        @pl.when(level == 0)
        def _():
            @pl.when(jnp.logical_or(m > 0, core == 1))
            def _():
                pl.semaphore_wait(turn, 1)

            for i in order:
                token_copy(i, m, res, rows).start()

            @pl.when(jnp.logical_and(m == micro - 1, core == 0))
            def _():
                token_copy(1, m, res, rows).wait_send()
                pl.semaphore_signal(turn, inc=1, device_id=sibling, device_id_type=MESH)

        return carry

    lax.fori_loop(0, micro, body, 0)

    for copy in started:
        copy.wait_send()

    def finish(m, carry):
        pltpu.make_async_copy(res.at[m], out_ref.at[m], out_sem.at[m]).wait()
        @pl.when(level == 0)
        def _():
            for i in (3, 0, 2):
                token_copy(i, m, res, rows).wait_send()

            @pl.when(jnp.logical_and(m == micro - 1, core == 1))
            def _():
                token_copy(1, m, res, rows).wait_send()

        for here, source, count in outgoing:

            @pl.when(level == here)
            def _():
                for i in order:
                    token_copy(i, m, source, count).wait_send()

        return carry

    lax.fori_loop(0, micro, finish, 0)


def shards(tokens_in, keep_one, keep_two, keep_three, norm_gain, layer_scale, w_qkv, w_out):
    micro, _, rows, feats = tokens_in.shape
    rows_in, rows_out = w_qkv.shape[1], w_out.shape[1]
    tiles = feats // LANE
    every, rest = compaction(rows_in, rows_out, tiles)
    pad_in = -(-8 * rows_in // 16) * 16
    pad_out = -(-8 * rows_out // 16) * 16
    vmem = pl.BlockSpec(memory_space=pltpu.VMEM)
    dma = pltpu.SemaphoreType.DMA
    stash = pl.pallas_call(
        kernel,
        out_shape=jax.ShapeDtypeStruct((micro, rows, feats), jnp.bfloat16),
        in_specs=[pl.BlockSpec(memory_space=pl.ANY)] + [vmem] * 7 + [pl.BlockSpec(memory_space=pl.ANY)] * 2,
        out_specs=pl.BlockSpec(memory_space=pl.ANY),
        scratch_shapes=[
            pltpu.VMEM((2, 8, 4, tiles * MAIN + REST, LANE), jnp.bfloat16),
            pltpu.VMEM((8, pad_in, feats), jnp.bfloat16),
            pltpu.VMEM((8, pad_out, feats), jnp.bfloat16),
            pltpu.VMEM((micro, rows, feats), jnp.bfloat16),
            pltpu.VMEM((micro, rows, feats), jnp.bfloat16),
            pltpu.VMEM((micro, rows, feats), jnp.bfloat16),
            pltpu.VMEM((micro, rows, rows), jnp.bfloat16),
            pltpu.VMEM((64, feats), jnp.float32),
            pltpu.VMEM((REST, LANE), jnp.float32),
            pltpu.VMEM((rows, feats), jnp.bfloat16),
            pltpu.VMEM((AHEAD * rows, feats), jnp.bfloat16),
            pltpu.VMEM((AHEAD, 64 * rows_in, rows), jnp.float32),
            pltpu.VMEM((64 * rows_out, rows), jnp.float32),
            pltpu.VMEM(every.shape, jnp.bfloat16),
            pltpu.VMEM(rest.shape, jnp.bfloat16),
            pltpu.VMEM((8 * pad_in, rows), jnp.float32),
            pltpu.VMEM((micro, 8, rows), jnp.float32),
            pltpu.VMEM((micro, 8, rows), jnp.float32),
            dma,
            dma((2,)),
            dma((micro,)),
            dma((2, 4, 4)),
            dma((2, 4, 4)),
            dma((2, 4)),
            dma((2, 4)),
            dma((2, 2)),
            dma((2, 2)),
            dma((8, 2, 2)),
            dma((8, 2, 2)),
            dma((8, 2)),
            dma((8, 2)),
            dma((4, micro)),
            dma((4, micro)),
            pltpu.SemaphoreType.REGULAR,
            pltpu.SemaphoreType.REGULAR,
        ],
        compiler_params=pltpu.CompilerParams(
            collective_id=0, has_side_effects=True, vmem_limit_bytes=60 * 1024 * 1024
        ),
    )(
        tokens_in[:, 0],
        keep_one[:, 0],
        keep_two[:, 0],
        keep_three[:, 0],
        norm_gain,
        layer_scale,
        w_qkv[0],
        w_out[0],
        jnp.asarray(every, jnp.bfloat16),
        jnp.asarray(rest, jnp.bfloat16),
    )
    return stash[None, :, None]


def solution(mesh):
    return jax.shard_map(
        shards,
        mesh=mesh,
        in_specs=(
            P(None, ("fsdp", "dp"), None, None),
            P(None, ("fsdp", "dp"), None),
            P(None, ("fsdp", "dp"), None),
            P(None, ("fsdp", "dp"), None),
            P("section", None),
            P("section", None),
            P("section", ("fsdp", "dp"), None),
            P("section", ("fsdp", "dp"), None),
        ),
        out_specs=P("section", None, ("fsdp", "dp"), None, None),
        check_vma=False,
    )
```
